512 devices in a mesh: video: 64 (over y_hi, x, z), mp: 8 (over y_lo, core).
Axes of the slice: x: 4, y: 8 (y_hi: 2, y_lo: 4; y = y_hi * 4 + y_lo), z: 8, core: 2. Of those that a mesh axis runs over, the one named last changes fastest.
Arguments:
- frames: bfloat16 [16384, 4096], P('video', 'mp'), may hold values from -36 to 36
- cotangent: bfloat16 [192, 128, 4096], P('video'), may hold values from -6 to 6
- w_qkv: bfloat16 [4096, 16, 384], P('video', 'mp'), as said below
- w_out: bfloat16 [128, 16, 4096], P('video', 'mp'), may hold values from -0.125 to 0.125
- starts: int32 [192], P('video'), may hold values from 0 to 255, as said below
- counts: int32 [64], P('video'), may hold values from 0 to 3
Outputs:
- frame_grads: float32 [16384, 4096], P('video', 'mp')
The draws below stay inside these ranges and needn't reach their ends.
Inputs may be any that keep to these rules, and one draw needn't show every extreme that they name: Windows lie inside the video: a slot of the last shard starts at most 128; slots of other shards may reach into the next shard; slots at or beyond their shard's count are unused. `w_qkv`: every entry lies within 4 / sqrt(4096) in magnitude.
All inputs are finite; a program needn't handle non-finite values.
Results may differ from the reference program's by a relative error of at most 0.014.
The reference program's roundings to bfloat16 on the way (of `window_rows`, `projected`, `attention_low`, `grad_heads`, `grad_values`, `grad_scores`, `grad_qkv` and `part`) count: a program that leaves them out, or rounds other values in their place, can miss the bound.
Values may be sent and summed in bfloat16 or wider, within the bound.
A program may use at most 64 MiB of HBM per device.

```python
import math
import jax
import jax.numpy as jnp
from jax import lax

MODEL_WIDTH = 4096
HEADS = 16
HD = 128
WINDOW_FRAMES = 128
FR_DEV = 256
CAP = 3
SHARDS = 64
NF = 16384
WINDOW_SLOTS = 192
N_MP = 8


def draw_frames(key, part):
    key = jax.random.fold_in(key, 5)
    first = jax.random.fold_in(key, 0)
    value_rows = jnp.clip(jax.random.normal(first, (NF, MODEL_WIDTH), jnp.float32), -6.0, 6.0)
    return value_rows.astype(jnp.bfloat16)


def draw_w_qkv(key, part):
    key = jax.random.fold_in(key, 7)
    value_rows = jnp.clip(jax.random.normal(key, (MODEL_WIDTH, HEADS, 3 * HD), jnp.float32), -4.0, 4.0) * MODEL_WIDTH ** (-0.5)
    return value_rows.astype(jnp.bfloat16)


def draw_starts(key, part):
    key = jax.random.fold_in(key, 11)
    first, second, third = jax.random.split(key, 3)
    value_rows = jax.random.randint(first, (SHARDS, CAP), 0, FR_DEV)
    closing = jax.random.randint(second, (SHARDS, CAP), 0, FR_DEV - WINDOW_FRAMES + 1)
    final = (jnp.arange(SHARDS) == SHARDS - 1)[:, None]
    value_rows = jnp.where(final, closing, value_rows)
    chosen = jax.random.randint(third, (), 0, SHARDS - 1)
    value_rows = value_rows.at[chosen, 0].set(FR_DEV - 1)
    value_rows = value_rows.at[(chosen + 1) % SHARDS, 0].set(0)
    return value_rows.reshape(WINDOW_SLOTS).astype(jnp.int32)


def draw_counts(key, part):
    key = jax.random.fold_in(key, 13)
    first, second, third = jax.random.split(key, 3)
    value_rows = jax.random.randint(first, (SHARDS,), 0, CAP + 1)
    busiest = jax.random.randint(second, (), 0, SHARDS)
    emptiest = (busiest + 1 + jax.random.randint(third, (), 0, SHARDS - 1)) % SHARDS
    value_rows = value_rows.at[busiest].set(CAP).at[emptiest].set(0)
    return value_rows.astype(jnp.int32)


def levels(stream_key, shape, pieces, smallest, high):
    gain, own = 1.0, jax.random.fold_in(stream_key, 6)
    for axis_at, blocks in pieces:
        draws = jnp.exp(jax.random.uniform(jax.random.fold_in(own, axis_at), (blocks,), jnp.float32, smallest / len(pieces), high / len(pieces)))
        gain = gain * jnp.repeat(draws, shape[axis_at] // blocks).reshape([-1 if axis == axis_at else 1 for axis in range(len(shape))])
    return gain


def bell_draw(key, dims, scale, bound, cuts=(), held_as=jnp.bfloat16):
    values = jax.random.normal(key, dims, jnp.float32) * scale
    if len(cuts) > 0:
        values = levels(key, dims, cuts, -0.22, 0.18) * values
    return jnp.clip(values, min=-bound, max=bound).astype(held_as)


def setup_inputs(seed: int = 0) -> dict:
    seeds = jax.random.split(jax.random.key(seed), 7)
    frames = draw_frames(jax.random.fold_in(seeds[6], 71), 0)
    cotangent = bell_draw(seeds[1], (WINDOW_SLOTS, WINDOW_FRAMES, MODEL_WIDTH), 1.0, 6.0, ((0, 64),))
    w_qkv = draw_w_qkv(jax.random.fold_in(seeds[6], 71), 0)
    w_out = bell_draw(seeds[3], (HD, HEADS, MODEL_WIDTH), (HEADS * HD) ** -0.5, 0.125, ((0, 64), (1, 8)))
    starts = draw_starts(jax.random.fold_in(seeds[6], 71), 0)
    counts = draw_counts(jax.random.fold_in(seeds[6], 71), 0)
    return {"frames": frames, "cotangent": cotangent, "w_qkv": w_qkv, "w_out": w_out, "starts": starts, "counts": counts}


def rounded(value_rows):
    return lax.optimization_barrier(value_rows.astype(jnp.bfloat16)).astype(jnp.float32)

def window_terms(window_rows, grad_rows, w_qkv, w_out):
    width = window_rows.shape[1]
    head_count = w_qkv.shape[1]
    head_size = w_qkv.shape[2] // 3
    scale = 1.0 / math.sqrt(head_size)
    projected = jnp.dot(window_rows, w_qkv.reshape(width, head_count * 3 * head_size), preferred_element_type=jnp.float32)
    projected = rounded(projected).reshape(window_rows.shape[0], head_count, 3 * head_size)
    queries = projected[..., :head_size]
    key_vectors = projected[..., head_size:2 * head_size]
    value_vectors = projected[..., 2 * head_size:]
    highest = lax.Precision.HIGHEST
    scores = jnp.einsum('qhe,khe->hqk', queries, key_vectors, precision=highest) * scale
    attention = jax.nn.softmax(scores, axis=-1)
    attention_low = rounded(attention)
    grad_heads = rounded(jnp.einsum('wd,ehd->whe', grad_rows.astype(jnp.float32), w_out.astype(jnp.float32), precision=highest))
    grad_values = rounded(jnp.einsum('hqk,qhe->khe', attention_low, grad_heads, precision=highest))
    grad_attention = jnp.einsum('qhe,khe->hqk', grad_heads, value_vectors, precision=highest)
    centre = lax.optimization_barrier(jnp.sum(attention * grad_attention, axis=-1, keepdims=True))
    grad_scores = rounded(attention * (grad_attention - centre) * scale)
    grad_queries = rounded(jnp.einsum('hqk,khe->qhe', grad_scores, key_vectors, precision=highest))
    grad_keys = rounded(jnp.einsum('hqk,qhe->khe', grad_scores, queries, precision=highest))
    grad_qkv = jnp.concatenate([grad_queries, grad_keys, grad_values], axis=-1)
    group_heads = head_count // N_MP
    grad_groups = grad_qkv.reshape(window_rows.shape[0], N_MP, group_heads, 3 * head_size)
    weight_groups = w_qkv.astype(jnp.float32).reshape(width, N_MP, group_heads, 3 * head_size)
    return jnp.einsum('wghe,dghe->gwd', grad_groups, weight_groups, precision=highest)

def reference(frames, cotangent, w_qkv, w_out, starts, counts):
    width = frames.shape[1]
    padded = jnp.concatenate([frames, jnp.zeros((WINDOW_FRAMES, width), jnp.bfloat16)], axis=0)
    total = jnp.zeros((NF + WINDOW_FRAMES, width), jnp.float32)

    def owner_step(total, owner):
        parts = jnp.zeros((N_MP, FR_DEV + WINDOW_FRAMES, width), jnp.float32)
        direct = jnp.zeros((FR_DEV + WINDOW_FRAMES, width), jnp.float32)
        for slot in range(CAP):
            index = owner * CAP + slot
            start = lax.dynamic_index_in_dim(starts, index, 0, keepdims=False).astype(jnp.int32)
            live = (slot < lax.dynamic_index_in_dim(counts, owner, 0, keepdims=False)).astype(jnp.float32)
            window_rows = lax.dynamic_slice_in_dim(padded, (owner * FR_DEV + start).astype(jnp.int32), WINDOW_FRAMES, 0)
            grad_rows = lax.dynamic_index_in_dim(cotangent, index, 0, keepdims=False)
            terms = window_terms(window_rows, grad_rows, w_qkv, w_out) * live
            placed = lax.dynamic_slice_in_dim(parts, start, WINDOW_FRAMES, 1) + terms
            parts = lax.dynamic_update_slice_in_dim(parts, placed, start, 1)
            placed_direct = lax.dynamic_slice_in_dim(direct, start, WINDOW_FRAMES, 0) + grad_rows.astype(jnp.float32) * live
            direct = lax.dynamic_update_slice_in_dim(direct, placed_direct, start, 0)
        merged = lax.optimization_barrier(jnp.sum(rounded(parts), axis=0)) + direct
        begin = (owner * FR_DEV).astype(jnp.int32)
        region = lax.dynamic_slice_in_dim(total, begin, FR_DEV + WINDOW_FRAMES, 0) + merged
        return (lax.dynamic_update_slice_in_dim(total, region, begin, 0), None)
    total, unused = lax.scan(owner_step, total, jnp.arange(SHARDS, dtype=jnp.int32))
    return total[:NF]
```

```python
import math

import jax
import jax.numpy as jnp
from jax import lax
from jax.experimental import pallas as pl
from jax.experimental.pallas import tpu as pltpu
from jax.sharding import PartitionSpec as P

HIGH, XS, ZS, LOW, CORES = 2, 4, 8, 4, 2
VIDEO = HIGH * XS * ZS
MP = LOW * CORES
MAX_COPIES = 160
MAX_LOCAL = 16
MESH = pl.DeviceIdType.MESH
NT = (((1,), (1,)), ((), ()))
TN = (((0,), (0,)), ((), ()))
F32, BF16 = jnp.float32, jnp.bfloat16


def dot(a, b, dims=(((1,), (0,)), ((), ()))):
    return lax.dot_general(a, b, dims, preferred_element_type=F32)


def kernel(
    starts, counts, frames, cotangent, first_shard, second_shard, out,
    wa, wb, ext, cot, wide, proj_a, proj_b, low, rows, heads, grads, placed,
    direct, own, give, take, part, summed, tail, tail_in, result,
    send_sems, recv_sems, local_sems,
):
    slots = starts.shape[0]
    frame_count, slab = frames.shape
    window = ext.shape[2] - frame_count
    total = ext.shape[2]
    shard_rows = first_shard.shape[0]
    size = proj_a.shape[1]
    qkv_b = proj_b.shape[1]
    piece = wa.shape[4] - size
    out_rows = wide.shape[1]
    scale = 1.0 / math.sqrt(size)

    video, mp = lax.axis_index("video"), lax.axis_index("mp")
    yh, x, z = video // (XS * ZS), (video // ZS) % XS, video % ZS
    yl, c = mp // CORES, mp % CORES
    other = 1 - yh
    xs = [(x + i) % XS for i in range(XS)]
    zs = [(z + i) % ZS for i in range(ZS)]
    yls = [(yl + i) % LOW for i in range(LOW)]
    before, after = (video + VIDEO - 1) % VIDEO, (video + 1) % VIDEO

    def at(video_at, mp_at):
        return {"video": video_at, "mp": mp_at}

    def place(yh_at, x_at, z_at):
        return (yh_at * XS + x_at) * ZS + z_at

    partner = at(place(other, x, z), mp)
    to_x = {1: at(place(yh, xs[1], z), mp), -1: at(place(yh, xs[-1], z), mp)}
    to_z = {1: at(place(yh, x, zs[1]), mp), -1: at(place(yh, x, zs[-1]), mp)}
    sibling = at(video, yl * CORES + 1 - c)

    met = [partner, to_x[1], to_x[-1], to_z[1], to_z[-1], sibling]
    met += [at(video, yls[d] * CORES + c) for d in range(1, LOW)]
    met += [at(side, yls[d] * CORES + c) for d in range(LOW) for side in (before, after)]
    barrier = pltpu.get_barrier_semaphore()
    for device in met:
        pl.semaphore_signal(barrier, inc=1, device_id=device, device_id_type=MESH)

    locals_ = []

    def stage(src, dst):
        copy = pltpu.make_async_copy(src, dst, local_sems.at[len(locals_)])
        copy.start()
        locals_.append(copy)
        return copy

    own_a = stage(first_shard, wa.at[yh, x, z])
    own_b = stage(second_shard, wb.at[yh, x, z])
    own_frames = stage(frames, ext.at[yl, c, pl.ds(0, frame_count)])
    cot_in = [stage(cotangent.at[:, pl.ds(u * slab, slab)], cot.at[u]) for u in range(MP)]

    pl.semaphore_wait(barrier, len(met))

    copies = []

    def push(src, dst, device):
        k = len(copies)
        copy = pltpu.make_async_remote_copy(
            src_ref=src, dst_ref=dst, send_sem=send_sems.at[k], recv_sem=recv_sems.at[k],
            device_id=device, device_id_type=MESH,
        )
        copy.start()
        copies.append(copy)
        return copy

    def same(ref, device):
        return push(ref, ref, device)

    dirs = (1, -1)

    pair_b = push(second_shard, wb.at[yh, x, z], partner)
    pair_a = push(first_shard, wa.at[yh, x, z], partner)
    bz, bx, az, ax, axf = {}, {}, {}, {}, {}
    for s in dirs:
        bz[s, 1] = [push(second_shard, wb.at[yh, x, z], to_z[s])]
    for s in dirs:
        ax[s] = [push(first_shard, wa.at[yh, x, z], to_x[s])]
    for s in dirs:
        bx[s, 0] = [push(second_shard, wb.at[yh, x, z], to_x[s])]

    body = pl.ds(0, frame_count)
    edge = pl.ds(frame_count, window)
    mine = ext.at[yl, c, body]
    far = {d: push(frames, mine, at(video, yls[d] * CORES + c)) for d in (2, 3, 1)}
    lent = {
        d: push(frames.at[pl.ds(0, window)], ext.at[yl, c, edge], at(before, yls[d] * CORES + c))
        for d in (2, 3, 1, 0)
    }

    pair_b.wait_recv()
    for s in dirs:
        bz[s, 1].append(same(wb.at[other, x, z], to_z[s]))
    pair_a.wait_recv()
    for s in dirs:
        ax[s].append(same(wa.at[other, x, z], to_x[s]))
    for s in dirs:
        bx[s, 0].append(same(wb.at[other, x, z], to_x[s]))

    def a_step(step, i):
        for s in dirs:
            z_at = zs[(-s * step) % ZS]
            if step < ZS // 2 - 1:
                ref = wa.at[:, xs[i], z_at]
            else:
                ref = wa.at[0 if s > 0 else 1, xs[i], z_at]
            az[s, step + 1, i] = same(ref, to_z[s])

    own_a.wait()
    a_step(0, 0)

    def b_arrive(step):
        for s in dirs:
            for copy in bz[s, step]:
                copy.wait_recv()
            z_at = zs[(-s * step) % ZS]
            if step < ZS // 2 - 1:
                bz[s, step + 1] = [same(wb.at[:, x, z_at], to_z[s])]
            elif step < ZS // 2:
                bz[s, step + 1] = [same(wb.at[0 if s > 0 else 1, x, z_at], to_z[s])]
        offsets = [-step % ZS, step % ZS] if step < ZS // 2 else [ZS // 2]
        for offset in offsets:
            for s in dirs:
                bx[s, offset] = [same(wb.at[:, x, zs[offset]], to_x[s])]

    bxf = {}

    def b_cross(offset):
        for s in dirs:
            for copy in bx[s, offset]:
                copy.wait_recv()
            ref = wb.at[0 if s > 0 else 1, xs[-s % XS], zs[offset]]
            bxf[s, offset] = same(ref, to_x[s])

    b_arrive(1)
    for s in dirs:
        for copy in ax[s]:
            copy.wait_recv()
        axf[s] = same(wa.at[0 if s > 0 else 1, xs[-s % XS], z], to_x[s])
    a_step(0, 1)
    a_step(0, 3)
    b_arrive(2)
    for s in dirs:
        axf[s].wait_recv()
    a_step(0, 2)
    own_b.wait()
    b_cross(0)
    b_arrive(3)
    b_arrive(4)

    order = (0, 1, 3, 2)

    def a_arrive(step, i):
        for s in dirs:
            az[s, step, i].wait_recv()
        a_step(step, i)

    def share(d):
        if d == 0:
            own_frames.wait()
        else:
            far[d].wait_recv()
        lent[d].wait_recv()
        return same(ext.at[yls[-d % LOW], c], sibling)

    shared = []
    b_cross(7)
    a_arrive(1, 0)
    b_cross(1)
    a_arrive(1, 1)
    a_arrive(1, 3)
    b_cross(6)
    a_arrive(1, 2)
    shared.append(share(0))
    b_cross(2)
    a_arrive(2, 0)
    a_arrive(2, 1)
    b_cross(5)
    shared.append(share(1))
    a_arrive(2, 3)
    b_cross(3)
    a_arrive(2, 2)
    b_cross(4)
    shared.append(share(3))
    for i in order:
        a_arrive(3, i)
    shared.append(share(2))

    for copy in cot_in:
        copy.wait()

    r = lax.broadcasted_iota(jnp.int32, (total, window), 0)
    w = lax.broadcasted_iota(jnp.int32, (total, window), 1)
    put = jnp.concatenate(
        [jnp.where((r - w == starts[j]) & (j < counts[0]), 1.0, 0.0).astype(BF16) for j in range(slots)],
        axis=1,
    )
    direct[...] = dot(put, cot[mp])

    for copy in shared:
        copy.wait_recv()
    for s in dirs:
        for i in order:
            az[s, ZS // 2, i].wait_recv()
        for offset in range(ZS):
            bxf[s, offset].wait_recv()

    proj_a[...] = jnp.zeros_like(proj_a)
    proj_b[...] = jnp.zeros_like(proj_b)

    @pl.loop(0, MP)
    def _(u):
        block = ext[u // CORES, u % CORES]
        weights_b = wb[u // XS, u % XS].reshape(ZS * shard_rows, qkv_b)
        weights_a = wa[u // XS, u % XS]
        proj_b[...] += dot(block, weights_b)
        proj_a[...] += dot(block, weights_a[:, :, :size].reshape(ZS * shard_rows, size))
        wide[pl.ds(u * ZS * 2, ZS * 2)] = (
            weights_a[:, :, size:].astype(F32).reshape(ZS * 2, out_rows, piece)
        )

    low[:, :qkv_b] = proj_b[...].astype(BF16)
    low[:, qkv_b:] = proj_a[...].astype(BF16)
    rows[...] = dot(put, low[...], TN).astype(BF16)

    parts = slab // piece
    count = MP * parts
    acc = jnp.zeros((slots * window, 2 * size), F32)
    for k in range(count):
        block = cot[k // parts, :, (k % parts) * piece:(k % parts + 1) * piece]
        weights = jnp.concatenate(
            [wide[:, h * count + k, :].astype(BF16) for h in range(2)], axis=0
        )
        acc += dot(block, weights, NT)
    heads[...] = acc.astype(BF16)

    for j in range(slots):
        span = slice(j * window, (j + 1) * window)
        for h in range(2):
            base = h * 3 * size
            queries = rows[span, base:base + size]
            keys = rows[span, base + size:base + 2 * size]
            values = rows[span, base + 2 * size:base + 3 * size]
            grad_head = heads[span, h * size:(h + 1) * size]
            scores = dot(queries, keys, NT) * scale
            powers = jnp.exp(scores - jnp.max(scores, axis=-1, keepdims=True))
            attention = powers / jnp.sum(powers, axis=-1, keepdims=True)
            grad_values = dot(attention.astype(BF16), grad_head, TN)
            grad_attention = dot(grad_head, values, NT)
            centre = jnp.sum(attention * grad_attention, axis=-1, keepdims=True)
            grad_scores = (attention * (grad_attention - centre) * scale).astype(BF16)
            grads[span, base:base + size] = dot(grad_scores, keys).astype(BF16)
            grads[span, base + size:base + 2 * size] = dot(grad_scores, queries, TN).astype(BF16)
            grads[span, base + 2 * size:base + 3 * size] = grad_values.astype(BF16)

    placed[...] = dot(put, grads[...]).astype(BF16)

    def group_part(yl_at, c_at):
        u = yl_at * CORES + c_at
        weights_b = wb[u // XS, u % XS].reshape(ZS * shard_rows, qkv_b)
        weights_a = wa[u // XS, u % XS, :, :, :size].reshape(ZS * shard_rows, size)
        return dot(placed[:, :qkv_b], weights_b, NT) + dot(placed[:, qkv_b:], weights_a, NT)

    sums = (2, 3, 1, 0)
    crossing = {}
    for d in sums:
        give[d] = group_part(yls[d], 1 - c).astype(BF16)
        crossing[d] = push(give.at[d], take.at[d], sibling)
    edges, bodies = {}, {}
    for d in sums:
        own[...] = group_part(yls[d], c).astype(BF16).astype(F32)
        crossing[d].wait_recv()
        if d == 0:
            direct[...] += own[...] + take[d].astype(F32)
        else:
            part[d - 1] = (own[...] + take[d].astype(F32)).astype(BF16)
            target = at(video, yls[d] * CORES + c)
            edges[d] = push(part.at[d - 1, edge], summed.at[d - 1, edge], target)
    for d in (2, 3, 1):
        target = at(video, yls[d] * CORES + c)
        bodies[d] = push(part.at[d - 1, body], summed.at[d - 1, body], target)
    for d in (2, 3, 1):
        edges[d].wait_recv()
    over = direct[frame_count:]
    for d in range(1, LOW):
        over += summed[d - 1, frame_count:].astype(F32)
    tail[...] = over.astype(BF16)
    carried = push(tail, tail_in, at(after, mp))
    for d in (2, 3, 1):
        bodies[d].wait_recv()
    keep = direct[:frame_count]
    for d in range(1, LOW):
        keep += summed[d - 1, :frame_count].astype(F32)
    result[...] = keep
    carried.wait_recv()
    result[:window] += jnp.where(video > 0, tail_in[...].astype(F32), 0.0)
    done = pltpu.make_async_copy(result, out, local_sems.at[MAX_LOCAL - 1])
    done.start()
    for copy in copies:
        copy.wait_send()
    done.wait()


def shards(frames, cotangent, w_qkv, w_out, starts, counts):
    frame_count, slab = frames.shape
    slots, window, width = cotangent.shape
    shard_rows, group, qkv = w_qkv.shape
    size = qkv // 3
    total = frame_count + window
    all_qkv = group * qkv
    qkv_b = all_qkv - size
    out_width = w_out.shape[0] * group * width // shard_rows
    flat = w_qkv.reshape(shard_rows, all_qkv)
    second = flat[:, :qkv_b]
    first = jnp.concatenate([flat[:, qkv_b:], w_out.reshape(shard_rows, out_width)], axis=1)
    out_rows = group * width // out_width
    smem = pl.BlockSpec(memory_space=pltpu.SMEM)
    hbm = pl.BlockSpec(memory_space=pl.ANY)
    vmem = pltpu.VMEM
    return pl.pallas_call(
        kernel,
        out_shape=jax.ShapeDtypeStruct((frame_count, slab), F32),
        in_specs=[smem, smem, hbm, hbm, hbm, hbm],
        out_specs=hbm,
        scratch_shapes=[
            vmem((HIGH, XS, ZS, shard_rows, size + out_width), BF16),
            vmem((HIGH, XS, ZS, shard_rows, qkv_b), BF16),
            vmem((LOW, CORES, total, slab), BF16),
            vmem((MP, slots * window, slab), BF16),
            vmem((size, out_rows, out_width), F32),
            vmem((total, size), F32),
            vmem((total, qkv_b), F32),
            vmem((total, all_qkv), BF16),
            vmem((slots * window, all_qkv), BF16),
            vmem((slots * window, group * size), BF16),
            vmem((slots * window, all_qkv), BF16),
            vmem((total, all_qkv), BF16),
            vmem((total, slab), F32),
            vmem((total, slab), F32),
            vmem((LOW, total, slab), BF16),
            vmem((LOW, total, slab), BF16),
            vmem((LOW - 1, total, slab), BF16),
            vmem((LOW - 1, total, slab), BF16),
            vmem((window, slab), BF16),
            vmem((window, slab), BF16),
            vmem((frame_count, slab), F32),
            pltpu.SemaphoreType.DMA((MAX_COPIES,)),
            pltpu.SemaphoreType.DMA((MAX_COPIES,)),
            pltpu.SemaphoreType.DMA((MAX_LOCAL,)),
        ],
        compiler_params=pltpu.CompilerParams(
            collective_id=0, has_side_effects=True, vmem_limit_bytes=56 * 2**20
        ),
    )(starts, counts, frames, cotangent.reshape(slots * window, width), first, second)


def solution(mesh):
    placed = (
        P("video", "mp"),
        P("video", None, None),
        P("video", "mp", None),
        P("video", "mp", None),
        P("video"),
        P("video"),
    )
    return jax.shard_map(
        shards, mesh=mesh, in_specs=placed, out_specs=P("video", "mp"), check_vma=False
    )
```

```python
import math

import jax
import jax.numpy as jnp
from jax import lax
from jax.experimental import pallas as pl
from jax.experimental.pallas import tpu as pltpu
from jax.sharding import PartitionSpec as P

HIGH, XS, ZS, LOW, CORES = 2, 4, 8, 4, 2
VIDEO = HIGH * XS * ZS
MP = LOW * CORES
MAX_COPIES = 128
MAX_MAYBE = 32
MAX_LOCAL = 16
MESH = pl.DeviceIdType.MESH
NT = (((1,), (1,)), ((), ()))
TN = (((0,), (0,)), ((), ()))
F32, BF16 = jnp.float32, jnp.bfloat16


def dot(a, b, dims=(((1,), (0,)), ((), ()))):
    return lax.dot_general(a, b, dims, preferred_element_type=F32)


def kernel(
    starts, counts, frames, cotangent, first_shard, second_shard, out,
    wa, wb, ext, cot, wide, proj_a, proj_b, low, rows, heads, grads, placed,
    direct, own, give, take, part, near, across, home, tail, tail_in, result,
    send_sems, recv_sems, local_sems,
):
    slots = starts.shape[0]
    frame_count, slab = frames.shape
    window = ext.shape[2] - frame_count
    total = ext.shape[2]
    shard_rows = first_shard.shape[0]
    size = proj_a.shape[1]
    qkv_b = proj_b.shape[1]
    piece = wa.shape[4] - size
    out_rows = wide.shape[1]
    scale = 1.0 / math.sqrt(size)

    video, mp = lax.axis_index("video"), lax.axis_index("mp")
    yh, x, z = video // (XS * ZS), (video // ZS) % XS, video % ZS
    yl, c = mp // CORES, mp % CORES
    other = 1 - yh
    xs = [(x + i) % XS for i in range(XS)]
    zs = [(z + i) % ZS for i in range(ZS)]
    yls = [(yl + i) % LOW for i in range(LOW)]
    before, after = (video + VIDEO - 1) % VIDEO, (video + 1) % VIDEO

    def at(video_at, mp_at):
        return {"video": video_at, "mp": mp_at}

    def place(yh_at, x_at, z_at):
        return (yh_at * XS + x_at) * ZS + z_at

    partner = at(place(other, x, z), mp)
    to_x = {1: at(place(yh, xs[1], z), mp), -1: at(place(yh, xs[-1], z), mp)}
    to_z = {1: at(place(yh, x, zs[1]), mp), -1: at(place(yh, x, zs[-1]), mp)}
    sibling = at(video, yl * CORES + 1 - c)

    last = LOW - 1
    lower = yl < LOW // 2
    line = [jnp.where(lower, b, last - b) for b in range(LOW)]
    is_end = (yl == 0) | (yl == last)
    is_mid = jnp.logical_not(is_end)
    outward = at(video, jnp.where(lower, yl + 1, yl - 1) * CORES + c)
    inward = at(video, jnp.where(lower, yl + last, yl + 1) % LOW * CORES + c)

    met = [partner, to_x[1], to_x[-1], to_z[1], to_z[-1], sibling]
    met += [at(video, yls[d] * CORES + c) for d in range(1, LOW)]
    met += [at(before, mp), at(after, mp)]
    barrier = pltpu.get_barrier_semaphore()
    for device in met:
        pl.semaphore_signal(barrier, inc=1, device_id=device, device_id_type=MESH)

    locals_ = []

    def stage(src, dst):
        copy = pltpu.make_async_copy(src, dst, local_sems.at[len(locals_)])
        copy.start()
        locals_.append(copy)
        return copy

    own_a = stage(first_shard, wa.at[yh, x, z])
    own_b = stage(second_shard, wb.at[yh, x, z])
    own_frames = stage(frames, ext.at[yl, c, pl.ds(0, frame_count)])
    cot_in = [stage(cotangent.at[:, pl.ds(u * slab, slab)], cot.at[u]) for u in range(MP)]

    pl.semaphore_wait(barrier, len(met))

    copies = []

    def push(src, dst, device):
        k = len(copies)
        copy = pltpu.make_async_remote_copy(
            src_ref=src, dst_ref=dst, send_sem=send_sems.at[k], recv_sem=recv_sems.at[k],
            device_id=device, device_id_type=MESH,
        )
        copy.start()
        copies.append(copy)
        return copy

    def same(ref, device):
        return push(ref, ref, device)

    dirs = (1, -1)

    pair_b = push(second_shard, wb.at[yh, x, z], partner)
    pair_a = push(first_shard, wa.at[yh, x, z], partner)
    bz, bx, az, ax, axf = {}, {}, {}, {}, {}
    for s in dirs:
        bz[s, 1] = [push(second_shard, wb.at[yh, x, z], to_z[s])]
    for s in dirs:
        ax[s] = [push(first_shard, wa.at[yh, x, z], to_x[s])]
    for s in dirs:
        bx[s, 0] = [push(second_shard, wb.at[yh, x, z], to_x[s])]

    body = pl.ds(0, frame_count)
    edge = pl.ds(frame_count, window)
    mine = ext.at[yl, c, body]
    lent = push(frames.at[pl.ds(0, window)], ext.at[yl, c, edge], at(before, mp))

    def later(src, dst, device):
        k = MAX_COPIES + len(maybe)
        copy = pltpu.make_async_remote_copy(
            src_ref=src, dst_ref=dst, send_sem=send_sems.at[k], recv_sem=recv_sems.at[k],
            device_id=device, device_id_type=MESH,
        )
        maybe.append(copy)
        return copy

    maybe = []
    end_out = [later(frames, mine, outward)]
    mid_out_f = [later(frames, mine, outward)]
    mid_in_f = [later(frames, mine, inward)]
    own_edge = ext.at[yl, c, edge]
    end_out.append(later(own_edge, own_edge, outward))
    mid_out_f.append(later(own_edge, own_edge, outward))
    mid_in_f.append(later(own_edge, own_edge, inward))
    pass_out, pass_mid, pass_far = (
        later(ext.at[line[b], c], ext.at[line[b], c], device)
        for b, device in ((0, outward), (2, inward), (3, inward))
    )

    def frame_start(i):
        @pl.when(is_end)
        def _():
            end_out[i].start()

        @pl.when(is_mid)
        def _():
            mid_in_f[i].start()
            mid_out_f[i].start()

    def frame_pass(i):
        @pl.when(is_mid)
        def _():
            if i == 0:
                for copy in end_out:
                    copy.wait_recv()
                pass_out.start()
                for copy in mid_out_f:
                    copy.wait_recv()
                pass_mid.start()
            else:
                pass_out.wait_recv()
                pass_far.start()

    frame_start(0)

    pair_b.wait_recv()
    for s in dirs:
        bz[s, 1].append(same(wb.at[other, x, z], to_z[s]))
    pair_a.wait_recv()
    for s in dirs:
        ax[s].append(same(wa.at[other, x, z], to_x[s]))
    for s in dirs:
        bx[s, 0].append(same(wb.at[other, x, z], to_x[s]))

    def a_step(step, i):
        for s in dirs:
            z_at = zs[(-s * step) % ZS]
            if step < ZS // 2 - 1:
                ref = wa.at[:, xs[i], z_at]
            else:
                ref = wa.at[0 if s > 0 else 1, xs[i], z_at]
            az[s, step + 1, i] = same(ref, to_z[s])

    own_a.wait()
    a_step(0, 0)
    lent.wait_recv()
    frame_start(1)

    def b_arrive(step):
        for s in dirs:
            for copy in bz[s, step]:
                copy.wait_recv()
            z_at = zs[(-s * step) % ZS]
            if step < ZS // 2 - 1:
                bz[s, step + 1] = [same(wb.at[:, x, z_at], to_z[s])]
            elif step < ZS // 2:
                bz[s, step + 1] = [same(wb.at[0 if s > 0 else 1, x, z_at], to_z[s])]
        offsets = [-step % ZS, step % ZS] if step < ZS // 2 else [ZS // 2]
        for offset in offsets:
            for s in dirs:
                bx[s, offset] = [same(wb.at[:, x, zs[offset]], to_x[s])]

    bxf = {}

    def b_cross(offset):
        for s in dirs:
            for copy in bx[s, offset]:
                copy.wait_recv()
            ref = wb.at[0 if s > 0 else 1, xs[-s % XS], zs[offset]]
            bxf[s, offset] = same(ref, to_x[s])

    b_arrive(1)
    for s in dirs:
        for copy in ax[s]:
            copy.wait_recv()
        axf[s] = same(wa.at[0 if s > 0 else 1, xs[-s % XS], z], to_x[s])
    a_step(0, 1)
    a_step(0, 3)
    b_arrive(2)
    frame_pass(0)
    for s in dirs:
        axf[s].wait_recv()
    a_step(0, 2)
    own_b.wait()
    b_cross(0)
    b_arrive(3)
    b_arrive(4)

    order = (0, 1, 3, 2)

    def a_arrive(step, i):
        for s in dirs:
            az[s, step, i].wait_recv()
        a_step(step, i)

    shared = []
    b_cross(7)
    a_arrive(1, 0)
    b_cross(1)
    frame_pass(1)
    a_arrive(1, 1)
    a_arrive(1, 3)
    b_cross(6)
    a_arrive(1, 2)
    b_cross(2)
    a_arrive(2, 0)
    a_arrive(2, 1)
    b_cross(5)
    a_arrive(2, 3)
    b_cross(3)
    a_arrive(2, 2)
    for i in order:
        a_arrive(3, i)
    b_cross(4)
    own_frames.wait()

    @pl.when(is_end)
    def _():
        for copy in mid_in_f:
            copy.wait_recv()
        pass_mid.wait_recv()
        pass_far.wait_recv()

    for b in range(LOW):
        shared.append(same(ext.at[line[b], c], sibling))

    for copy in cot_in:
        copy.wait()

    r = lax.broadcasted_iota(jnp.int32, (total, window), 0)
    w = lax.broadcasted_iota(jnp.int32, (total, window), 1)
    put = jnp.concatenate(
        [jnp.where((r - w == starts[j]) & (j < counts[0]), 1.0, 0.0).astype(BF16) for j in range(slots)],
        axis=1,
    )
    direct[...] = dot(put, cot[mp])

    for s in dirs:
        for i in order:
            az[s, ZS // 2, i].wait_recv()

    @pl.loop(0, MP)
    def _(u):
        weights = wa[u // XS, u % XS, :, :, size:]
        wide[pl.ds(u * ZS * 2, ZS * 2)] = (
            weights.astype(F32).reshape(ZS * 2, out_rows, piece)
        )

    parts = slab // piece
    count = MP * parts
    acc = jnp.zeros((slots * window, 2 * size), F32)
    for k in range(count):
        block = cot[k // parts, :, (k % parts) * piece:(k % parts + 1) * piece]
        weights = jnp.concatenate(
            [wide[:, h * count + k, :].astype(BF16) for h in range(2)], axis=0
        )
        acc += dot(block, weights, NT)
    heads[...] = acc.astype(BF16)

    for copy in shared:
        copy.wait_recv()
    for s in dirs:
        for offset in range(ZS):
            bxf[s, offset].wait_recv()

    proj_a[...] = jnp.zeros_like(proj_a)
    proj_b[...] = jnp.zeros_like(proj_b)

    @pl.loop(0, MP)
    def _(u):
        block = ext[u // CORES, u % CORES]
        weights_b = wb[u // XS, u % XS].reshape(ZS * shard_rows, qkv_b)
        weights_a = wa[u // XS, u % XS, :, :, :size].reshape(ZS * shard_rows, size)
        proj_b[...] += dot(block, weights_b)
        proj_a[...] += dot(block, weights_a)

    low[:, :qkv_b] = proj_b[...].astype(BF16)
    low[:, qkv_b:] = proj_a[...].astype(BF16)
    rows[...] = dot(put, low[...], TN).astype(BF16)

    for j in range(slots):
        span = slice(j * window, (j + 1) * window)
        for h in range(2):
            base = h * 3 * size
            queries = rows[span, base:base + size]
            keys = rows[span, base + size:base + 2 * size]
            values = rows[span, base + 2 * size:base + 3 * size]
            grad_head = heads[span, h * size:(h + 1) * size]
            scores = dot(queries, keys, NT) * scale
            powers = jnp.exp(scores - jnp.max(scores, axis=-1, keepdims=True))
            attention = powers / jnp.sum(powers, axis=-1, keepdims=True)
            grad_values = dot(attention.astype(BF16), grad_head, TN)
            grad_attention = dot(grad_head, values, NT)
            centre = jnp.sum(attention * grad_attention, axis=-1, keepdims=True)
            grad_scores = (attention * (grad_attention - centre) * scale).astype(BF16)
            grads[span, base:base + size] = dot(grad_scores, keys).astype(BF16)
            grads[span, base + size:base + 2 * size] = dot(grad_scores, queries, TN).astype(BF16)
            grads[span, base + 2 * size:base + 3 * size] = grad_values.astype(BF16)

    placed[...] = dot(put, grads[...]).astype(BF16)

    def group_part(yl_at, c_at):
        u = yl_at * CORES + c_at
        weights_b = wb[u // XS, u % XS].reshape(ZS * shard_rows, qkv_b)
        weights_a = wa[u // XS, u % XS, :, :, :size].reshape(ZS * shard_rows, size)
        return dot(placed[:, :qkv_b], weights_b, NT) + dot(placed[:, qkv_b:], weights_a, NT)

    chunks = (edge, body)
    from_end = [[later(part.at[b, t], near.at[b - 1, t], outward) for b in (1, 2, 3)] for t in chunks]
    from_mid = [[later(part.at[b, t], across.at[3 - b, t], outward) for b in (3, 2)] for t in chunks]
    to_end = [later(part.at[0, t], home.at[t], inward) for t in chunks]

    crossing = {}

    def cross(b):
        give[b] = group_part(line[b], 1 - c).astype(BF16)
        crossing[b] = push(give.at[b], take.at[b], sibling)

    def merge(b):
        own[...] = group_part(line[b], c).astype(BF16).astype(F32)
        crossing[b].wait_recv()
        own[...] += take[b].astype(F32)
        part[b] = own[...].astype(BF16)
        if b < 2:
            @pl.when(is_end if b == 0 else is_mid)
            def _():
                direct[...] += own[...]

    def end_send(*pairs):
        @pl.when(is_end)
        def _():
            for t, b in pairs:
                from_end[t][b - 1].start()

    cross(3)
    cross(2)
    merge(3)
    end_send((1, 3))
    cross(1)
    merge(2)
    end_send((0, 3), (0, 2))
    cross(0)
    merge(1)
    end_send((0, 1), (1, 2), (1, 1))

    def add(ref, t, other_ref):
        ref[...] = (ref[...].astype(F32) + other_ref[...].astype(F32)).astype(BF16)

    def mid_out(t, b):
        from_end[t][b - 1].wait_recv()
        add(part.at[b, chunks[t]], t, near.at[b - 1, chunks[t]])
        from_mid[t][3 - b].start()

    def mid_in(t):
        from_mid[t][0].wait_recv()
        add(part.at[0, chunks[t]], t, across.at[0, chunks[t]])
        to_end[t].start()

    def finish(t):
        @pl.when(is_end)
        def _():
            to_end[t].wait_recv()
            direct[chunks[t]] += home[chunks[t]].astype(F32)

        @pl.when(is_mid)
        def _():
            from_mid[t][1].wait_recv()
            from_end[t][0].wait_recv()
            direct[chunks[t]] += (
                near[0, chunks[t]].astype(F32) + across[1, chunks[t]].astype(F32)
            )

    @pl.when(is_mid)
    def _():
        mid_out(1, 3)
        mid_out(0, 3)

    merge(0)

    @pl.when(is_mid)
    def _():
        mid_out(0, 2)
        mid_in(0)

    finish(0)
    tail[...] = direct[frame_count:].astype(BF16)
    carried = push(tail, tail_in, at(after, mp))

    @pl.when(is_mid)
    def _():
        mid_in(1)
        mid_out(1, 2)

    finish(1)
    carried.wait_recv()
    result[...] = direct[:frame_count]
    result[:window] += jnp.where(video > 0, tail_in[...].astype(F32), 0.0)
    done = pltpu.make_async_copy(result, out, local_sems.at[MAX_LOCAL - 1])
    done.start()
    for copy in copies:
        copy.wait_send()
    @pl.when(is_end)
    def _():
        for t in range(2):
            for copy in from_end[t]:
                copy.wait_send()
            end_out[t].wait_send()

    @pl.when(is_mid)
    def _():
        for t in range(2):
            for copy in from_mid[t]:
                copy.wait_send()
            to_end[t].wait_send()
            mid_out_f[t].wait_send()
            mid_in_f[t].wait_send()
        for copy in (pass_out, pass_mid, pass_far):
            copy.wait_send()

    done.wait()


def shards(frames, cotangent, w_qkv, w_out, starts, counts):
    frame_count, slab = frames.shape
    slots, window, width = cotangent.shape
    shard_rows, group, qkv = w_qkv.shape
    size = qkv // 3
    total = frame_count + window
    all_qkv = group * qkv
    qkv_b = all_qkv - size
    out_width = w_out.shape[0] * group * width // shard_rows
    flat = w_qkv.reshape(shard_rows, all_qkv)
    second = flat[:, :qkv_b]
    first = jnp.concatenate([flat[:, qkv_b:], w_out.reshape(shard_rows, out_width)], axis=1)
    out_rows = group * width // out_width
    smem = pl.BlockSpec(memory_space=pltpu.SMEM)
    hbm = pl.BlockSpec(memory_space=pl.ANY)
    vmem = pltpu.VMEM
    return pl.pallas_call(
        kernel,
        out_shape=jax.ShapeDtypeStruct((frame_count, slab), F32),
        in_specs=[smem, smem, hbm, hbm, hbm, hbm],
        out_specs=hbm,
        scratch_shapes=[
            vmem((HIGH, XS, ZS, shard_rows, size + out_width), BF16),
            vmem((HIGH, XS, ZS, shard_rows, qkv_b), BF16),
            vmem((LOW, CORES, total, slab), BF16),
            vmem((MP, slots * window, slab), BF16),
            vmem((size, out_rows, out_width), F32),
            vmem((total, size), F32),
            vmem((total, qkv_b), F32),
            vmem((total, all_qkv), BF16),
            vmem((slots * window, all_qkv), BF16),
            vmem((slots * window, group * size), BF16),
            vmem((slots * window, all_qkv), BF16),
            vmem((total, all_qkv), BF16),
            vmem((total, slab), F32),
            vmem((total, slab), F32),
            vmem((LOW, total, slab), BF16),
            vmem((LOW, total, slab), BF16),
            vmem((LOW, total, slab), BF16),
            vmem((LOW - 1, total, slab), BF16),
            vmem((2, total, slab), BF16),
            vmem((total, slab), BF16),
            vmem((window, slab), BF16),
            vmem((window, slab), BF16),
            vmem((frame_count, slab), F32),
            pltpu.SemaphoreType.DMA((MAX_COPIES + MAX_MAYBE,)),
            pltpu.SemaphoreType.DMA((MAX_COPIES + MAX_MAYBE,)),
            pltpu.SemaphoreType.DMA((MAX_LOCAL,)),
        ],
        compiler_params=pltpu.CompilerParams(
            collective_id=0, has_side_effects=True, vmem_limit_bytes=56 * 2**20
        ),
    )(starts, counts, frames, cotangent.reshape(slots * window, width), first, second)


def solution(mesh):
    placed = (
        P("video", "mp"),
        P("video", None, None),
        P("video", "mp", None),
        P("video", "mp", None),
        P("video"),
        P("video"),
    )
    return jax.shard_map(
        shards, mesh=mesh, in_specs=placed, out_specs=P("video", "mp"), check_vma=False
    )
```

```python
import math

import jax
import jax.numpy as jnp
from jax import lax
from jax.experimental import pallas as pl
from jax.experimental.pallas import tpu as pltpu
from jax.sharding import PartitionSpec as P

HIGH, XS, ZS, LOW, CORES = 2, 4, 8, 4, 2
VIDEO = HIGH * XS * ZS
MP = LOW * CORES
MAX_COPIES = 128
MAX_MAYBE = 32
MAX_LOCAL = 16
MESH = pl.DeviceIdType.MESH
NT = (((1,), (1,)), ((), ()))
TN = (((0,), (0,)), ((), ()))
F32, BF16 = jnp.float32, jnp.bfloat16


def dot(a, b, dims=(((1,), (0,)), ((), ()))):
    return lax.dot_general(a, b, dims, preferred_element_type=F32)


def kernel(
    starts, counts, frames, cotangent, first_shard, second_shard, out,
    wa, wb, ext, cot, wide, proj_a, proj_b, low, rows, heads, grads, placed,
    direct, own, give, take, part, near, across, home, tail, tail_in, result,
    send_sems, recv_sems, local_sems,
):
    slots = starts.shape[0]
    frame_count, slab = frames.shape
    window = ext.shape[2] - frame_count
    total = ext.shape[2]
    shard_rows = first_shard.shape[0]
    size = proj_a.shape[1]
    qkv_b = proj_b.shape[1]
    piece = wa.shape[4] - size
    out_rows = wide.shape[1]
    scale = 1.0 / math.sqrt(size)

    video, mp = lax.axis_index("video"), lax.axis_index("mp")
    yh, x, z = video // (XS * ZS), (video // ZS) % XS, video % ZS
    yl, c = mp // CORES, mp % CORES
    other = 1 - yh
    xs = [(x + i) % XS for i in range(XS)]
    zs = [(z + i) % ZS for i in range(ZS)]
    yls = [(yl + i) % LOW for i in range(LOW)]
    before, after = (video + VIDEO - 1) % VIDEO, (video + 1) % VIDEO

    def at(video_at, mp_at):
        return {"video": video_at, "mp": mp_at}

    def place(yh_at, x_at, z_at):
        return (yh_at * XS + x_at) * ZS + z_at

    partner = at(place(other, x, z), mp)
    to_x = {1: at(place(yh, xs[1], z), mp), -1: at(place(yh, xs[-1], z), mp)}
    to_z = {1: at(place(yh, x, zs[1]), mp), -1: at(place(yh, x, zs[-1]), mp)}
    sibling = at(video, yl * CORES + 1 - c)

    last = LOW - 1
    lower = yl < LOW // 2
    line = [jnp.where(lower, b, last - b) for b in range(LOW)]
    is_end = (yl == 0) | (yl == last)
    is_mid = jnp.logical_not(is_end)
    outward = at(video, jnp.where(lower, yl + 1, yl - 1) * CORES + c)
    inward = at(video, jnp.where(lower, yl + last, yl + 1) % LOW * CORES + c)

    met = [partner, to_x[1], to_x[-1], to_z[1], to_z[-1], sibling]
    met += [at(video, yls[d] * CORES + c) for d in range(1, LOW)]
    met += [at(before, mp), at(after, mp)]
    barrier = pltpu.get_barrier_semaphore()
    for device in met:
        pl.semaphore_signal(barrier, inc=1, device_id=device, device_id_type=MESH)

    locals_ = []

    def stage(src, dst):
        copy = pltpu.make_async_copy(src, dst, local_sems.at[len(locals_)])
        copy.start()
        locals_.append(copy)
        return copy

    own_a = stage(first_shard, wa.at[yh, x, z])
    own_b = stage(second_shard, wb.at[yh, x, z])
    own_frames = stage(frames, ext.at[yl, c, pl.ds(0, frame_count)])
    cot_in = [stage(cotangent.at[:, pl.ds(u * slab, slab)], cot.at[u]) for u in range(MP)]

    pl.semaphore_wait(barrier, len(met))

    copies = []

    def push(src, dst, device):
        k = len(copies)
        copy = pltpu.make_async_remote_copy(
            src_ref=src, dst_ref=dst, send_sem=send_sems.at[k], recv_sem=recv_sems.at[k],
            device_id=device, device_id_type=MESH,
        )
        copy.start()
        copies.append(copy)
        return copy

    def same(ref, device):
        return push(ref, ref, device)

    dirs = (1, -1)

    pair_b = push(second_shard, wb.at[yh, x, z], partner)
    pair_a = push(first_shard, wa.at[yh, x, z], partner)
    bz, bx, az, ax, axf = {}, {}, {}, {}, {}
    for s in dirs:
        bz[s, 1] = [push(second_shard, wb.at[yh, x, z], to_z[s])]
    for s in dirs:
        ax[s] = [push(first_shard, wa.at[yh, x, z], to_x[s])]
    for s in dirs:
        bx[s, 0] = [push(second_shard, wb.at[yh, x, z], to_x[s])]

    body = pl.ds(0, frame_count)
    edge = pl.ds(frame_count, window)
    mine = ext.at[yl, c, body]
    def later(src, dst, device):
        k = MAX_COPIES + len(maybe)
        copy = pltpu.make_async_remote_copy(
            src_ref=src, dst_ref=dst, send_sem=send_sems.at[k], recv_sem=recv_sems.at[k],
            device_id=device, device_id_type=MESH,
        )
        maybe.append(copy)
        return copy

    maybe = []
    first, final = video == 0, video == VIDEO - 1
    lent = later(frames.at[pl.ds(0, window)], ext.at[yl, c, edge], at(before, mp))

    @pl.when(jnp.logical_not(first))
    def _():
        lent.start()

    end_out = [later(frames, mine, outward)]
    mid_out_f = [later(frames, mine, outward)]
    mid_in_f = [later(frames, mine, inward)]
    own_edge = ext.at[yl, c, edge]
    end_out.append(later(own_edge, own_edge, outward))
    mid_out_f.append(later(own_edge, own_edge, outward))
    mid_in_f.append(later(own_edge, own_edge, inward))
    pass_out, pass_mid, pass_far = (
        later(ext.at[line[b], c], ext.at[line[b], c], device)
        for b, device in ((0, outward), (2, inward), (3, inward))
    )

    def frame_start(i):
        @pl.when(is_end)
        def _():
            end_out[i].start()

        @pl.when(is_mid)
        def _():
            mid_in_f[i].start()
            mid_out_f[i].start()

    def frame_pass(i):
        @pl.when(is_mid)
        def _():
            if i == 0:
                for copy in end_out:
                    copy.wait_recv()
                pass_out.start()
                for copy in mid_out_f:
                    copy.wait_recv()
                pass_mid.start()
            else:
                pass_out.wait_recv()
                pass_far.start()

    frame_start(0)

    def b_early(q, i):
        for s in dirs:
            bz[s, 1][i].wait_recv()
            ref = wb.at[q, x, zs[-s % ZS]]
            bz.setdefault((s, 2), []).append(same(ref, to_z[s]))
        for s in dirs:
            ref = wb.at[q, x, zs[-s % ZS]]
            for side in dirs:
                bx.setdefault((side, -s % ZS), []).append(same(ref, to_x[side]))

    b_early(yh, 0)
    pair_b.wait_recv()
    for s in dirs:
        bz[s, 1].append(same(wb.at[other, x, z], to_z[s]))
    pair_a.wait_recv()
    for s in dirs:
        ax[s].append(same(wa.at[other, x, z], to_x[s]))
    for s in dirs:
        bx[s, 0].append(same(wb.at[other, x, z], to_x[s]))

    def widen(i, z_at):
        for h in range(HIGH):
            block = wa[h, xs[i], z_at, :, size:].astype(F32)
            spot = pl.ds(2 * place(h, xs[i], z_at), 2)
            wide[spot] = block.reshape(2, out_rows, piece)

    def a_step(step, i):
        for s in dirs:
            z_at = zs[(-s * step) % ZS]
            if step < ZS // 2 - 1:
                ref = wa.at[:, xs[i], z_at]
            else:
                ref = wa.at[0 if s > 0 else 1, xs[i], z_at]
            az[s, step + 1, i] = same(ref, to_z[s])

    own_a.wait()
    a_step(0, 0)

    @pl.when(jnp.logical_not(final))
    def _():
        lent.wait_recv()

    @pl.when(final)
    def _():
        ext[yl, c, frame_count:] = jnp.zeros((window, slab), BF16)

    frame_start(1)

    def b_arrive(step):
        for s in dirs:
            for copy in bz[s, step]:
                copy.wait_recv()
            z_at = zs[(-s * step) % ZS]
            if step < ZS // 2 - 1:
                bz[s, step + 1] = [same(wb.at[:, x, z_at], to_z[s])]
            elif step < ZS // 2:
                bz[s, step + 1] = [same(wb.at[0 if s > 0 else 1, x, z_at], to_z[s])]
        offsets = [-step % ZS, step % ZS] if step < ZS // 2 else [ZS // 2]
        for offset in offsets:
            for s in dirs:
                bx[s, offset] = [same(wb.at[:, x, zs[offset]], to_x[s])]

    bxf = {}

    def b_cross(offset):
        for s in dirs:
            for copy in bx[s, offset]:
                copy.wait_recv()
            ref = wb.at[0 if s > 0 else 1, xs[-s % XS], zs[offset]]
            bxf[s, offset] = same(ref, to_x[s])

    b_early(other, 1)
    for s in dirs:
        for copy in ax[s]:
            copy.wait_recv()
        axf[s] = same(wa.at[0 if s > 0 else 1, xs[-s % XS], z], to_x[s])
    a_step(0, 1)
    a_step(0, 3)
    for i in (0, 1, 3):
        widen(i, z)
    b_arrive(2)
    frame_pass(0)
    for s in dirs:
        axf[s].wait_recv()
    a_step(0, 2)
    widen(2, z)
    own_b.wait()
    b_cross(0)
    b_arrive(3)
    b_arrive(4)

    order = (0, 1, 3, 2)

    def a_arrive(step, i):
        for s in dirs:
            az[s, step, i].wait_recv()
        a_step(step, i)
        for s in dirs:
            widen(i, zs[-s * step % ZS])

    shared = []
    b_cross(7)
    a_arrive(1, 0)
    b_cross(1)
    frame_pass(1)
    a_arrive(1, 1)
    a_arrive(1, 3)
    b_cross(6)
    a_arrive(1, 2)
    b_cross(2)
    a_arrive(2, 0)
    a_arrive(2, 1)
    b_cross(5)
    a_arrive(2, 3)
    b_cross(3)
    a_arrive(2, 2)
    own_frames.wait()

    @pl.when(is_end)
    def _():
        for copy in mid_in_f:
            copy.wait_recv()
        pass_mid.wait_recv()
        pass_far.wait_recv()

    for b in range(LOW):
        shared.append(same(ext.at[line[b], c], sibling))

    for i in order:
        a_arrive(3, i)
    b_cross(4)

    for copy in cot_in:
        copy.wait()

    r = lax.broadcasted_iota(jnp.int32, (total, window), 0)
    w = lax.broadcasted_iota(jnp.int32, (total, window), 1)
    put = jnp.concatenate(
        [jnp.where((r - w == starts[j]) & (j < counts[0]), 1.0, 0.0).astype(BF16) for j in range(slots)],
        axis=1,
    )
    direct[...] = dot(put, cot[mp])

    for copy in shared:
        copy.wait_recv()

    proj_a[...] = jnp.zeros_like(proj_a)
    proj_b[...] = jnp.zeros_like(proj_b)

    def project_b(i):
        @pl.loop(0, HIGH)
        def _(h):
            u = h * XS + xs[i]
            weights = wb[h, xs[i]].reshape(ZS * shard_rows, qkv_b)
            proj_b[...] += dot(ext[u // CORES, u % CORES], weights)

    for i in (0, 1, 3):
        project_b(i)

    for s in dirs:
        for i in order:
            az[s, ZS // 2, i].wait_recv()
    for i in order:
        widen(i, zs[ZS // 2])

    @pl.loop(0, MP)
    def _(u):
        weights = wa[u // XS, u % XS, :, :, :size].reshape(ZS * shard_rows, size)
        proj_a[...] += dot(ext[u // CORES, u % CORES], weights)

    parts = slab // piece
    count = MP * parts
    acc = jnp.zeros((slots * window, 2 * size), F32)
    for k in range(count):
        block = cot[k // parts, :, (k % parts) * piece:(k % parts + 1) * piece]
        weights = jnp.concatenate(
            [wide[:, h * count + k, :].astype(BF16) for h in range(2)], axis=0
        )
        acc += dot(block, weights, NT)
    heads[...] = acc.astype(BF16)

    for s in dirs:
        for offset in range(ZS):
            bxf[s, offset].wait_recv()
    project_b(2)

    low[:, :qkv_b] = proj_b[...].astype(BF16)
    low[:, qkv_b:] = proj_a[...].astype(BF16)
    rows[...] = dot(put, low[...], TN).astype(BF16)

    for j in range(slots):
        span = slice(j * window, (j + 1) * window)
        for h in range(2):
            base = h * 3 * size
            queries = rows[span, base:base + size]
            keys = rows[span, base + size:base + 2 * size]
            values = rows[span, base + 2 * size:base + 3 * size]
            grad_head = heads[span, h * size:(h + 1) * size]
            scores = dot(queries, keys, NT) * scale
            powers = jnp.exp(scores - jnp.max(scores, axis=-1, keepdims=True))
            attention = powers / jnp.sum(powers, axis=-1, keepdims=True)
            grad_values = dot(attention.astype(BF16), grad_head, TN)
            grad_attention = dot(grad_head, values, NT)
            centre = jnp.sum(attention * grad_attention, axis=-1, keepdims=True)
            grad_scores = (attention * (grad_attention - centre) * scale).astype(BF16)
            grads[span, base:base + size] = dot(grad_scores, keys).astype(BF16)
            grads[span, base + size:base + 2 * size] = dot(grad_scores, queries, TN).astype(BF16)
            grads[span, base + 2 * size:base + 3 * size] = grad_values.astype(BF16)

    placed[...] = dot(put, grads[...]).astype(BF16)

    def group_part(yl_at, c_at):
        u = yl_at * CORES + c_at
        weights_b = wb[u // XS, u % XS].reshape(ZS * shard_rows, qkv_b)
        weights_a = wa[u // XS, u % XS, :, :, :size].reshape(ZS * shard_rows, size)
        return dot(placed[:, :qkv_b], weights_b, NT) + dot(placed[:, qkv_b:], weights_a, NT)

    chunks = (edge, body)
    from_end = [[later(part.at[b, t], near.at[b - 1, t], outward) for b in (1, 2, 3)] for t in chunks]
    from_mid = [[later(part.at[b, t], across.at[3 - b, t], outward) for b in (3, 2)] for t in chunks]
    to_end = [later(part.at[0, t], home.at[t], inward) for t in chunks]

    crossing = {}

    def cross(b):
        give[b] = group_part(line[b], 1 - c).astype(BF16)
        crossing[b] = push(give.at[b], take.at[b], sibling)

    def merge(b):
        own[...] = group_part(line[b], c).astype(BF16).astype(F32)
        crossing[b].wait_recv()
        own[...] += take[b].astype(F32)
        part[b] = own[...].astype(BF16)
        if b < 2:
            @pl.when(is_end if b == 0 else is_mid)
            def _():
                direct[...] += own[...]

    def end_send(*pairs):
        @pl.when(is_end)
        def _():
            for t, b in pairs:
                from_end[t][b - 1].start()

    cross(3)
    cross(2)
    merge(3)
    end_send((0, 3))
    cross(1)
    merge(2)
    end_send((0, 2))
    cross(0)
    merge(1)
    end_send((0, 1), (1, 3), (1, 2), (1, 1))

    def add(ref, t, other_ref):
        ref[...] = (ref[...].astype(F32) + other_ref[...].astype(F32)).astype(BF16)

    def mid_out(t, b):
        from_end[t][b - 1].wait_recv()
        add(part.at[b, chunks[t]], t, near.at[b - 1, chunks[t]])
        from_mid[t][3 - b].start()

    def mid_in(t):
        from_mid[t][0].wait_recv()
        add(part.at[0, chunks[t]], t, across.at[0, chunks[t]])
        to_end[t].start()

    def finish(t):
        @pl.when(is_end)
        def _():
            to_end[t].wait_recv()
            direct[chunks[t]] += home[chunks[t]].astype(F32)

        @pl.when(is_mid)
        def _():
            from_mid[t][1].wait_recv()
            from_end[t][0].wait_recv()
            direct[chunks[t]] += (
                near[0, chunks[t]].astype(F32) + across[1, chunks[t]].astype(F32)
            )

    merge(0)

    @pl.when(is_mid)
    def _():
        mid_out(0, 3)
        mid_out(0, 2)
        mid_in(0)

    finish(0)
    tail[...] = direct[frame_count:].astype(BF16)
    carried = later(tail, tail_in, at(after, mp))

    @pl.when(jnp.logical_not(final))
    def _():
        carried.start()

    @pl.when(is_mid)
    def _():
        mid_out(1, 3)
        mid_in(1)
        mid_out(1, 2)

    finish(1)
    result[...] = direct[:frame_count]

    @pl.when(jnp.logical_not(first))
    def _():
        carried.wait_recv()
        result[:window] += tail_in[...].astype(F32)

    done = pltpu.make_async_copy(result, out, local_sems.at[MAX_LOCAL - 1])
    done.start()
    for copy in copies:
        copy.wait_send()

    @pl.when(jnp.logical_not(first))
    def _():
        lent.wait_send()

    @pl.when(jnp.logical_not(final))
    def _():
        carried.wait_send()

    @pl.when(is_end)
    def _():
        for t in range(2):
            for copy in from_end[t]:
                copy.wait_send()
            end_out[t].wait_send()

    @pl.when(is_mid)
    def _():
        for t in range(2):
            for copy in from_mid[t]:
                copy.wait_send()
            to_end[t].wait_send()
            mid_out_f[t].wait_send()
            mid_in_f[t].wait_send()
        for copy in (pass_out, pass_mid, pass_far):
            copy.wait_send()

    done.wait()


def shards(frames, cotangent, w_qkv, w_out, starts, counts):
    frame_count, slab = frames.shape
    slots, window, width = cotangent.shape
    shard_rows, group, qkv = w_qkv.shape
    size = qkv // 3
    total = frame_count + window
    all_qkv = group * qkv
    qkv_b = all_qkv - size
    out_width = w_out.shape[0] * group * width // shard_rows
    flat = w_qkv.reshape(shard_rows, all_qkv)
    second = flat[:, :qkv_b]
    first = jnp.concatenate([flat[:, qkv_b:], w_out.reshape(shard_rows, out_width)], axis=1)
    out_rows = group * width // out_width
    smem = pl.BlockSpec(memory_space=pltpu.SMEM)
    hbm = pl.BlockSpec(memory_space=pl.ANY)
    vmem = pltpu.VMEM
    return pl.pallas_call(
        kernel,
        out_shape=jax.ShapeDtypeStruct((frame_count, slab), F32),
        in_specs=[smem, smem, hbm, hbm, hbm, hbm],
        out_specs=hbm,
        scratch_shapes=[
            vmem((HIGH, XS, ZS, shard_rows, size + out_width), BF16),
            vmem((HIGH, XS, ZS, shard_rows, qkv_b), BF16),
            vmem((LOW, CORES, total, slab), BF16),
            vmem((MP, slots * window, slab), BF16),
            vmem((size, out_rows, out_width), F32),
            vmem((total, size), F32),
            vmem((total, qkv_b), F32),
            vmem((total, all_qkv), BF16),
            vmem((slots * window, all_qkv), BF16),
            vmem((slots * window, group * size), BF16),
            vmem((slots * window, all_qkv), BF16),
            vmem((total, all_qkv), BF16),
            vmem((total, slab), F32),
            vmem((total, slab), F32),
            vmem((LOW, total, slab), BF16),
            vmem((LOW, total, slab), BF16),
            vmem((LOW, total, slab), BF16),
            vmem((LOW - 1, total, slab), BF16),
            vmem((2, total, slab), BF16),
            vmem((total, slab), BF16),
            vmem((window, slab), BF16),
            vmem((window, slab), BF16),
            vmem((frame_count, slab), F32),
            pltpu.SemaphoreType.DMA((MAX_COPIES + MAX_MAYBE,)),
            pltpu.SemaphoreType.DMA((MAX_COPIES + MAX_MAYBE,)),
            pltpu.SemaphoreType.DMA((MAX_LOCAL,)),
        ],
        compiler_params=pltpu.CompilerParams(
            collective_id=0, has_side_effects=True, vmem_limit_bytes=56 * 2**20
        ),
    )(starts, counts, frames, cotangent.reshape(slots * window, width), first, second)


def solution(mesh):
    placed = (
        P("video", "mp"),
        P("video", None, None),
        P("video", "mp", None),
        P("video", "mp", None),
        P("video"),
        P("video"),
    )
    return jax.shard_map(
        shards, mesh=mesh, in_specs=placed, out_specs=P("video", "mp"), check_vma=False
    )
```

```python
import math

import jax
import jax.numpy as jnp
from jax import lax
from jax.experimental import pallas as pl
from jax.experimental.pallas import tpu as pltpu
from jax.sharding import PartitionSpec as P

HIGH, XS, ZS, LOW, CORES = 2, 4, 8, 4, 2
VIDEO = HIGH * XS * ZS
MP = LOW * CORES
MAX_COPIES = 128
MAX_MAYBE = 32
MAX_LOCAL = 16
MESH = pl.DeviceIdType.MESH
NT = (((1,), (1,)), ((), ()))
TN = (((0,), (0,)), ((), ()))
F32, BF16 = jnp.float32, jnp.bfloat16


def dot(a, b, dims=(((1,), (0,)), ((), ()))):
    return lax.dot_general(a, b, dims, preferred_element_type=F32)


def kernel(
    starts, counts, frames, cotangent, first_shard, second_shard, out,
    wa, wb, ext, cot, wide, order_rows, proj_a, proj_b, low, rows, heads, grads, placed,
    direct, own, give, take, part, near, across, home, tail, tail_in, result,
    send_sems, recv_sems, local_sems,
):
    slots = starts.shape[0]
    frame_count, slab = frames.shape
    window = ext.shape[2] - frame_count
    total = ext.shape[2]
    shard_rows = first_shard.shape[0]
    size = proj_a.shape[1]
    qkv_b = proj_b.shape[1]
    piece = wa.shape[4] - size
    out_rows = 2 * wide.shape[0]
    scale = 1.0 / math.sqrt(size)

    video, mp = lax.axis_index("video"), lax.axis_index("mp")
    yh, x, z = video // (XS * ZS), (video // ZS) % XS, video % ZS
    yl, c = mp // CORES, mp % CORES
    other = 1 - yh
    xs = [(x + i) % XS for i in range(XS)]
    zs = [(z + i) % ZS for i in range(ZS)]
    yls = [(yl + i) % LOW for i in range(LOW)]
    before, after = (video + VIDEO - 1) % VIDEO, (video + 1) % VIDEO

    def at(video_at, mp_at):
        return {"video": video_at, "mp": mp_at}

    def place(yh_at, x_at, z_at):
        return (yh_at * XS + x_at) * ZS + z_at

    partner = at(place(other, x, z), mp)
    to_x = {1: at(place(yh, xs[1], z), mp), -1: at(place(yh, xs[-1], z), mp)}
    to_z = {1: at(place(yh, x, zs[1]), mp), -1: at(place(yh, x, zs[-1]), mp)}
    sibling = at(video, yl * CORES + 1 - c)

    last = LOW - 1
    lower = yl < LOW // 2
    line = [jnp.where(lower, b, last - b) for b in range(LOW)]
    is_end = (yl == 0) | (yl == last)
    is_mid = jnp.logical_not(is_end)
    outward = at(video, jnp.where(lower, yl + 1, yl - 1) * CORES + c)
    inward = at(video, jnp.where(lower, yl + last, yl + 1) % LOW * CORES + c)

    met = [partner, to_x[1], to_x[-1], to_z[1], to_z[-1], sibling]
    met += [at(video, yls[d] * CORES + c) for d in range(1, LOW)]
    met += [at(before, mp), at(after, mp)]
    barrier = pltpu.get_barrier_semaphore()
    for device in met:
        pl.semaphore_signal(barrier, inc=1, device_id=device, device_id_type=MESH)

    locals_ = []

    def stage(src, dst):
        copy = pltpu.make_async_copy(src, dst, local_sems.at[len(locals_)])
        copy.start()
        locals_.append(copy)
        return copy

    own_a = stage(first_shard, wa.at[yh, x, z])
    own_b = stage(second_shard, wb.at[yh, x, z])
    own_frames = stage(frames, ext.at[yl, c, pl.ds(0, frame_count)])
    cot_in = [stage(cotangent.at[:, pl.ds(u * slab, slab)], cot.at[u]) for u in range(MP)]

    pl.semaphore_wait(barrier, len(met))

    copies = []

    def push(src, dst, device):
        k = len(copies)
        copy = pltpu.make_async_remote_copy(
            src_ref=src, dst_ref=dst, send_sem=send_sems.at[k], recv_sem=recv_sems.at[k],
            device_id=device, device_id_type=MESH,
        )
        copy.start()
        copies.append(copy)
        return copy

    def same(ref, device):
        return push(ref, ref, device)

    dirs = (1, -1)

    pair_b = push(second_shard, wb.at[yh, x, z], partner)
    pair_a = push(first_shard, wa.at[yh, x, z], partner)
    bz, bx, az, ax, axf = {}, {}, {}, {}, {}
    for s in dirs:
        bz[s, 1] = [push(second_shard, wb.at[yh, x, z], to_z[s])]
    for s in dirs:
        ax[s] = [push(first_shard, wa.at[yh, x, z], to_x[s])]
    for s in dirs:
        bx[s, 0] = [push(second_shard, wb.at[yh, x, z], to_x[s])]

    body = pl.ds(0, frame_count)
    edge = pl.ds(frame_count, window)
    mine = ext.at[yl, c, body]
    def later(src, dst, device):
        k = MAX_COPIES + len(maybe)
        copy = pltpu.make_async_remote_copy(
            src_ref=src, dst_ref=dst, send_sem=send_sems.at[k], recv_sem=recv_sems.at[k],
            device_id=device, device_id_type=MESH,
        )
        maybe.append(copy)
        return copy

    maybe = []
    first, final = video == 0, video == VIDEO - 1
    lent = later(frames.at[pl.ds(0, window)], ext.at[yl, c, edge], at(before, mp))

    @pl.when(jnp.logical_not(first))
    def _():
        lent.start()

    end_out = [later(frames, mine, outward)]
    mid_out_f = [later(frames, mine, outward)]
    mid_in_f = [later(frames, mine, inward)]
    own_edge = ext.at[yl, c, edge]
    end_out.append(later(own_edge, own_edge, outward))
    mid_out_f.append(later(own_edge, own_edge, outward))
    mid_in_f.append(later(own_edge, own_edge, inward))
    pass_out, pass_mid, pass_far = (
        later(ext.at[line[b], c], ext.at[line[b], c], device)
        for b, device in ((0, outward), (2, inward), (3, inward))
    )

    def frame_start(i):
        @pl.when(is_end)
        def _():
            end_out[i].start()

        @pl.when(is_mid)
        def _():
            mid_in_f[i].start()
            mid_out_f[i].start()

    def frame_pass(i):
        @pl.when(is_mid)
        def _():
            if i == 0:
                for copy in end_out:
                    copy.wait_recv()
                pass_out.start()
                for copy in mid_out_f:
                    copy.wait_recv()
                pass_mid.start()
            else:
                pass_out.wait_recv()
                pass_far.start()

    def b_early(q, i):
        for s in dirs:
            bz[s, 1][i].wait_recv()
            ref = wb.at[q, x, zs[-s % ZS]]
            bz.setdefault((s, 2), []).append(same(ref, to_z[s]))
        for s in dirs:
            ref = wb.at[q, x, zs[-s % ZS]]
            for side in dirs:
                bx.setdefault((side, -s % ZS), []).append(same(ref, to_x[side]))

    b_early(yh, 0)
    frame_start(0)
    pair_b.wait_recv()
    for s in dirs:
        bz[s, 1].append(same(wb.at[other, x, z], to_z[s]))
    pair_a.wait_recv()
    for s in dirs:
        ax[s].append(same(wa.at[other, x, z], to_x[s]))
    for s in dirs:
        bx[s, 0].append(same(wb.at[other, x, z], to_x[s]))

    group = HIGH * XS
    per_shard = shard_rows // out_rows
    half = out_rows // 2
    mixed = group * shard_rows
    to = lax.broadcasted_iota(jnp.int32, (mixed, mixed), 0)
    source = lax.broadcasted_iota(jnp.int32, (mixed, mixed), 1)
    each = 2 * group * per_shard
    inner = to % (group * per_shard)
    wanted = (
        inner // per_shard * shard_rows + inner % per_shard * out_rows
        + to % each // (group * per_shard) * half + to // each
    )
    order_rows[...] = jnp.where(source == wanted, 1.0, 0.0).astype(BF16)

    def sort(z_at):
        block = wa[:, :, z_at, :, size:].reshape(mixed, piece)
        wide[:, z_at] = dot(order_rows[...], block).astype(BF16).reshape(half, each, piece)

    def a_step(step, i):
        for s in dirs:
            z_at = zs[(-s * step) % ZS]
            if step < ZS // 2 - 1:
                ref = wa.at[:, xs[i], z_at]
            else:
                ref = wa.at[0 if s > 0 else 1, xs[i], z_at]
            az[s, step + 1, i] = same(ref, to_z[s])

    own_a.wait()
    a_step(0, 0)

    @pl.when(jnp.logical_not(final))
    def _():
        lent.wait_recv()

    @pl.when(final)
    def _():
        ext[yl, c, frame_count:] = jnp.zeros((window, slab), BF16)

    frame_start(1)

    def b_arrive(step):
        for s in dirs:
            for copy in bz[s, step]:
                copy.wait_recv()
            z_at = zs[(-s * step) % ZS]
            if step < ZS // 2 - 1:
                bz[s, step + 1] = [same(wb.at[:, x, z_at], to_z[s])]
            elif step < ZS // 2:
                bz[s, step + 1] = [same(wb.at[0 if s > 0 else 1, x, z_at], to_z[s])]
        offsets = [-step % ZS, step % ZS] if step < ZS // 2 else [ZS // 2]
        for offset in offsets:
            for s in dirs:
                bx[s, offset] = [same(wb.at[:, x, zs[offset]], to_x[s])]

    bxf = {}

    def b_cross(offset):
        for s in dirs:
            for copy in bx[s, offset]:
                copy.wait_recv()
            ref = wb.at[0 if s > 0 else 1, xs[-s % XS], zs[offset]]
            bxf[s, offset] = same(ref, to_x[s])

    order = (0, 1, 3, 2)

    def a_arrive(step, i):
        for s in dirs:
            az[s, step, i].wait_recv()
        a_step(step, i)

    shared = []
    b_early(other, 1)
    for s in dirs:
        for copy in ax[s]:
            copy.wait_recv()
        axf[s] = same(wa.at[0 if s > 0 else 1, xs[-s % XS], z], to_x[s])
    a_step(0, 1)
    a_step(0, 3)
    frame_pass(0)
    b_arrive(2)
    a_arrive(1, 0)
    for s in dirs:
        axf[s].wait_recv()
    a_step(0, 2)
    b_cross(0)
    sort(z)
    own_b.wait()
    b_arrive(3)
    a_arrive(1, 1)
    b_cross(7)
    a_arrive(1, 3)
    b_arrive(4)
    frame_pass(1)
    b_cross(1)
    a_arrive(1, 2)
    a_arrive(2, 0)
    b_cross(6)
    sort(zs[1])
    sort(zs[-1])
    a_arrive(2, 1)
    b_cross(2)
    a_arrive(2, 3)
    own_frames.wait()

    @pl.when(is_end)
    def _():
        for copy in mid_in_f:
            copy.wait_recv()
        pass_mid.wait_recv()

    for copy in cot_in:
        copy.wait()

    r = lax.broadcasted_iota(jnp.int32, (total, window), 0)
    w = lax.broadcasted_iota(jnp.int32, (total, window), 1)
    put = jnp.concatenate(
        [jnp.where((r - w == starts[j]) & (j < counts[0]), 1.0, 0.0).astype(BF16) for j in range(slots)],
        axis=1,
    )
    direct[...] = dot(put, cot[mp])


    def project_b(i, h):
        u = h * XS + xs[i]
        weights = wb[h, xs[i]].reshape(ZS * shard_rows, qkv_b)
        proj_b[...] += dot(ext[u // CORES, u % CORES], weights)

    for b in range(LOW - 1):
        shared.append(same(ext.at[line[b], c], sibling))
    b_cross(5)
    a_arrive(2, 2)
    sort(zs[2])
    sort(zs[-2])
    b_cross(3)
    a_arrive(3, 0)
    b_cross(4)

    @pl.when(is_end)
    def _():
        pass_far.wait_recv()

    shared.append(same(ext.at[line[LOW - 1], c], sibling))
    proj_a[...] = jnp.zeros_like(proj_a)
    proj_b[...] = jnp.zeros_like(proj_b)
    a_arrive(3, 1)
    for copy in shared:
        copy.wait_recv()
    project_b(0, 0)
    project_b(0, 1)
    a_arrive(3, 3)
    project_b(1, 0)
    a_arrive(3, 2)
    sort(zs[3])
    sort(zs[-3])
    project_b(1, 1)
    project_b(3, 0)
    project_b(3, 1)


    for s in dirs:
        for i in order:
            az[s, ZS // 2, i].wait_recv()
    sort(zs[ZS // 2])

    @pl.loop(0, MP)
    def _(u):
        weights = wa[u // XS, u % XS, :, :, :size].reshape(ZS * shard_rows, size)
        proj_a[...] += dot(ext[u // CORES, u % CORES], weights)

    parts = slab // piece
    acc = jnp.zeros((slots * window, ZS * each), F32)
    for k in range(half):
        block = cot[k // parts, :, (k % parts) * piece:(k % parts + 1) * piece]
        acc += dot(block, wide[k].reshape(ZS * each, piece), NT)
    n = lax.broadcasted_iota(jnp.int32, (ZS * each, ZS * each), 0)
    n_to = lax.broadcasted_iota(jnp.int32, (ZS * each, ZS * each), 1)
    inner = n % (group * per_shard)
    wanted = (
        n % each // (group * per_shard) * size
        + (inner // per_shard * ZS + n // each) * per_shard + inner % per_shard
    )
    columns = jnp.where(n_to == wanted, 1.0, 0.0).astype(BF16)
    heads[...] = dot(acc.astype(BF16), columns).astype(BF16)

    for s in dirs:
        for offset in range(ZS):
            bxf[s, offset].wait_recv()
    for h in range(HIGH):
        project_b(2, h)

    low[:, :qkv_b] = proj_b[...].astype(BF16)
    low[:, qkv_b:] = proj_a[...].astype(BF16)
    rows[...] = dot(put, low[...], TN).astype(BF16)

    for j in range(slots):
        span = slice(j * window, (j + 1) * window)
        for h in range(2):
            base = h * 3 * size
            queries = rows[span, base:base + size]
            keys = rows[span, base + size:base + 2 * size]
            values = rows[span, base + 2 * size:base + 3 * size]
            grad_head = heads[span, h * size:(h + 1) * size]
            scores = dot(queries, keys, NT) * scale
            powers = jnp.exp(scores - jnp.max(scores, axis=-1, keepdims=True))
            attention = powers / jnp.sum(powers, axis=-1, keepdims=True)
            grad_values = dot(attention.astype(BF16), grad_head, TN)
            grad_attention = dot(grad_head, values, NT)
            centre = jnp.sum(attention * grad_attention, axis=-1, keepdims=True)
            grad_scores = (attention * (grad_attention - centre) * scale).astype(BF16)
            grads[span, base:base + size] = dot(grad_scores, keys).astype(BF16)
            grads[span, base + size:base + 2 * size] = dot(grad_scores, queries, TN).astype(BF16)
            grads[span, base + 2 * size:base + 3 * size] = grad_values.astype(BF16)

    placed[...] = dot(put, grads[...]).astype(BF16)

    def group_part(yl_at, c_at):
        u = yl_at * CORES + c_at
        weights_b = wb[u // XS, u % XS].reshape(ZS * shard_rows, qkv_b)
        weights_a = wa[u // XS, u % XS, :, :, :size].reshape(ZS * shard_rows, size)
        return dot(placed[:, :qkv_b], weights_b, NT) + dot(placed[:, qkv_b:], weights_a, NT)

    chunks = (edge, body)
    from_end = [[later(part.at[b, t], near.at[b - 1, t], outward) for b in (1, 2, 3)] for t in chunks]
    from_mid = [[later(part.at[b, t], across.at[3 - b, t], outward) for b in (3, 2)] for t in chunks]
    to_end = [later(part.at[0, t], home.at[t], inward) for t in chunks]

    crossing = {}

    def cross(b):
        give[b] = group_part(line[b], 1 - c).astype(BF16)
        crossing[b] = push(give.at[b], take.at[b], sibling)

    def merge(b):
        own[...] = group_part(line[b], c).astype(BF16).astype(F32)
        crossing[b].wait_recv()
        own[...] += take[b].astype(F32)
        part[b] = own[...].astype(BF16)
        if b < 2:
            @pl.when(is_end if b == 0 else is_mid)
            def _():
                direct[...] += own[...]

    def end_send(*pairs):
        @pl.when(is_end)
        def _():
            for t, b in pairs:
                from_end[t][b - 1].start()

    cross(3)
    cross(2)
    merge(3)
    end_send((0, 3))
    cross(1)
    merge(2)
    end_send((0, 2))
    cross(0)
    merge(1)
    end_send((0, 1), (1, 3), (1, 2), (1, 1))

    def add(ref, t, other_ref):
        ref[...] = (ref[...].astype(F32) + other_ref[...].astype(F32)).astype(BF16)

    def mid_out(t, b):
        from_end[t][b - 1].wait_recv()
        add(part.at[b, chunks[t]], t, near.at[b - 1, chunks[t]])
        from_mid[t][3 - b].start()

    def mid_in(t):
        from_mid[t][0].wait_recv()
        add(part.at[0, chunks[t]], t, across.at[0, chunks[t]])
        to_end[t].start()

    def finish(t):
        @pl.when(is_end)
        def _():
            to_end[t].wait_recv()
            direct[chunks[t]] += home[chunks[t]].astype(F32)

        @pl.when(is_mid)
        def _():
            from_mid[t][1].wait_recv()
            from_end[t][0].wait_recv()
            direct[chunks[t]] += (
                near[0, chunks[t]].astype(F32) + across[1, chunks[t]].astype(F32)
            )

    merge(0)

    @pl.when(is_mid)
    def _():
        mid_out(0, 3)
        mid_out(0, 2)
        mid_in(0)

    finish(0)
    tail[...] = direct[frame_count:].astype(BF16)
    carried = later(tail, tail_in, at(after, mp))

    @pl.when(jnp.logical_not(final))
    def _():
        carried.start()

    @pl.when(is_mid)
    def _():
        mid_out(1, 3)
        mid_in(1)
        mid_out(1, 2)

    finish(1)
    result[...] = direct[:frame_count]

    @pl.when(jnp.logical_not(first))
    def _():
        carried.wait_recv()
        result[:window] += tail_in[...].astype(F32)

    done = pltpu.make_async_copy(result, out, local_sems.at[MAX_LOCAL - 1])
    done.start()
    for copy in copies:
        copy.wait_send()

    @pl.when(jnp.logical_not(first))
    def _():
        lent.wait_send()

    @pl.when(jnp.logical_not(final))
    def _():
        carried.wait_send()

    @pl.when(is_end)
    def _():
        for t in range(2):
            for copy in from_end[t]:
                copy.wait_send()
            end_out[t].wait_send()

    @pl.when(is_mid)
    def _():
        for t in range(2):
            for copy in from_mid[t]:
                copy.wait_send()
            to_end[t].wait_send()
            mid_out_f[t].wait_send()
            mid_in_f[t].wait_send()
        for copy in (pass_out, pass_mid, pass_far):
            copy.wait_send()

    done.wait()


def shards(frames, cotangent, w_qkv, w_out, starts, counts):
    frame_count, slab = frames.shape
    slots, window, width = cotangent.shape
    shard_rows, group, qkv = w_qkv.shape
    size = qkv // 3
    total = frame_count + window
    all_qkv = group * qkv
    qkv_b = all_qkv - size
    out_width = w_out.shape[0] * group * width // shard_rows
    flat = w_qkv.reshape(shard_rows, all_qkv)
    second = flat[:, :qkv_b]
    first = jnp.concatenate([flat[:, qkv_b:], w_out.reshape(shard_rows, out_width)], axis=1)
    out_rows = group * width // out_width
    smem = pl.BlockSpec(memory_space=pltpu.SMEM)
    hbm = pl.BlockSpec(memory_space=pl.ANY)
    vmem = pltpu.VMEM
    return pl.pallas_call(
        kernel,
        out_shape=jax.ShapeDtypeStruct((frame_count, slab), F32),
        in_specs=[smem, smem, hbm, hbm, hbm, hbm],
        out_specs=hbm,
        scratch_shapes=[
            vmem((HIGH, XS, ZS, shard_rows, size + out_width), BF16),
            vmem((HIGH, XS, ZS, shard_rows, qkv_b), BF16),
            vmem((LOW, CORES, total, slab), BF16),
            vmem((MP, slots * window, slab), BF16),
            vmem((out_rows // 2, ZS, 2 * HIGH * XS * shard_rows // out_rows, out_width), BF16),
            vmem((HIGH * XS * shard_rows, HIGH * XS * shard_rows), BF16),
            vmem((total, size), F32),
            vmem((total, qkv_b), F32),
            vmem((total, all_qkv), BF16),
            vmem((slots * window, all_qkv), BF16),
            vmem((slots * window, group * size), BF16),
            vmem((slots * window, all_qkv), BF16),
            vmem((total, all_qkv), BF16),
            vmem((total, slab), F32),
            vmem((total, slab), F32),
            vmem((LOW, total, slab), BF16),
            vmem((LOW, total, slab), BF16),
            vmem((LOW, total, slab), BF16),
            vmem((LOW - 1, total, slab), BF16),
            vmem((2, total, slab), BF16),
            vmem((total, slab), BF16),
            vmem((window, slab), BF16),
            vmem((window, slab), BF16),
            vmem((frame_count, slab), F32),
            pltpu.SemaphoreType.DMA((MAX_COPIES + MAX_MAYBE,)),
            pltpu.SemaphoreType.DMA((MAX_COPIES + MAX_MAYBE,)),
            pltpu.SemaphoreType.DMA((MAX_LOCAL,)),
        ],
        compiler_params=pltpu.CompilerParams(
            collective_id=0, has_side_effects=True, vmem_limit_bytes=56 * 2**20
        ),
    )(starts, counts, frames, cotangent.reshape(slots * window, width), first, second)


def solution(mesh):
    placed = (
        P("video", "mp"),
        P("video", None, None),
        P("video", "mp", None),
        P("video", "mp", None),
        P("video"),
        P("video"),
    )
    return jax.shard_map(
        shards, mesh=mesh, in_specs=placed, out_specs=P("video", "mp"), check_vma=False
    )
```

```python
import math

import jax
import jax.numpy as jnp
from jax import lax
from jax.experimental import pallas as pl
from jax.experimental.pallas import tpu as pltpu
from jax.sharding import PartitionSpec as P

HIGH, XS, ZS, LOW, CORES = 2, 4, 8, 4, 2
VIDEO = HIGH * XS * ZS
MP = LOW * CORES
MAX_COPIES = 128
MAX_MAYBE = 32
MAX_LOCAL = 16
MESH = pl.DeviceIdType.MESH
NT = (((1,), (1,)), ((), ()))
TN = (((0,), (0,)), ((), ()))
F32, BF16 = jnp.float32, jnp.bfloat16


def dot(a, b, dims=(((1,), (0,)), ((), ()))):
    return lax.dot_general(a, b, dims, preferred_element_type=F32)


def kernel(
    starts, counts, frames, cotangent, w_qkv, w_out, out,
    first_shard, second_shard, lines, wa, wb, ext, cot, wide, order_rows, proj_a, proj_b, low, rows, heads, grads, placed,
    direct, own, give, take, part, near, across, home, tail, tail_in, result,
    send_sems, recv_sems, local_sems,
):
    slots = starts.shape[0]
    frame_count, slab = frames.shape
    window = ext.shape[2] - frame_count
    total = ext.shape[2]
    shard_rows = w_qkv.shape[0]
    size = proj_a.shape[1]
    qkv_b = proj_b.shape[1]
    piece = wa.shape[4] - size
    out_rows = 2 * wide.shape[0]
    scale = 1.0 / math.sqrt(size)

    video, mp = lax.axis_index("video"), lax.axis_index("mp")
    yh, x, z = video // (XS * ZS), (video // ZS) % XS, video % ZS
    yl, c = mp // CORES, mp % CORES
    other = 1 - yh
    xs = [(x + i) % XS for i in range(XS)]
    zs = [(z + i) % ZS for i in range(ZS)]
    yls = [(yl + i) % LOW for i in range(LOW)]
    before, after = (video + VIDEO - 1) % VIDEO, (video + 1) % VIDEO

    def at(video_at, mp_at):
        return {"video": video_at, "mp": mp_at}

    def place(yh_at, x_at, z_at):
        return (yh_at * XS + x_at) * ZS + z_at

    partner = at(place(other, x, z), mp)
    to_x = {1: at(place(yh, xs[1], z), mp), -1: at(place(yh, xs[-1], z), mp)}
    to_z = {1: at(place(yh, x, zs[1]), mp), -1: at(place(yh, x, zs[-1]), mp)}
    sibling = at(video, yl * CORES + 1 - c)

    last = LOW - 1
    lower = yl < LOW // 2
    line = [jnp.where(lower, b, last - b) for b in range(LOW)]
    is_end = (yl == 0) | (yl == last)
    is_mid = jnp.logical_not(is_end)
    outward = at(video, jnp.where(lower, yl + 1, yl - 1) * CORES + c)
    inward = at(video, jnp.where(lower, yl + last, yl + 1) % LOW * CORES + c)

    met = [partner, to_x[1], to_x[-1], to_z[1], to_z[-1], sibling]
    met += [at(video, yls[d] * CORES + c) for d in range(1, LOW)]
    met += [at(before, mp), at(after, mp)]
    barrier = pltpu.get_barrier_semaphore()
    for device in met:
        pl.semaphore_signal(barrier, inc=1, device_id=device, device_id_type=MESH)

    locals_ = []

    def stage(src, dst):
        copy = pltpu.make_async_copy(src, dst, local_sems.at[len(locals_)])
        copy.start()
        locals_.append(copy)
        return copy

    own_frames = stage(frames, ext.at[yl, c, pl.ds(0, frame_count)])
    cot_in = [stage(cotangent.at[:, pl.ds(u * slab, slab)], cot.at[u]) for u in range(MP)]

    qkv = w_qkv[...].astype(F32)
    panels = w_out[...].astype(F32)
    head_qkv = 3 * size
    second_shard[:, :head_qkv] = qkv[:, 0].astype(BF16)
    second_shard[:, head_qkv:] = qkv[:, 1, :qkv_b - head_qkv].astype(BF16)
    first_shard[:, :size] = qkv[:, 1, qkv_b - head_qkv:].astype(BF16)
    for e in range(panels.shape[0]):
        for h in range(2):
            for k in range(out_rows // 2):
                row = (e * 2 + h) * (out_rows // 2) + k
                lines[row:row + 1] = panels[e, h:h + 1, k * piece:(k + 1) * piece]
    first_shard[:, size:] = lines[...].astype(BF16)
    own_a = stage(first_shard, wa.at[yh, x, z])
    own_b = stage(second_shard, wb.at[yh, x, z])

    pl.semaphore_wait(barrier, len(met))

    copies = []

    def push(src, dst, device):
        k = len(copies)
        copy = pltpu.make_async_remote_copy(
            src_ref=src, dst_ref=dst, send_sem=send_sems.at[k], recv_sem=recv_sems.at[k],
            device_id=device, device_id_type=MESH,
        )
        copy.start()
        copies.append(copy)
        return copy

    def same(ref, device):
        return push(ref, ref, device)

    dirs = (1, -1)

    pair_b = push(second_shard, wb.at[yh, x, z], partner)
    pair_a = push(first_shard, wa.at[yh, x, z], partner)
    bz, bx, az, ax, axf = {}, {}, {}, {}, {}
    for s in dirs:
        bz[s, 1] = [push(second_shard, wb.at[yh, x, z], to_z[s])]
    for s in dirs:
        ax[s] = [push(first_shard, wa.at[yh, x, z], to_x[s])]
    for s in dirs:
        bx[s, 0] = [push(second_shard, wb.at[yh, x, z], to_x[s])]

    body = pl.ds(0, frame_count)
    edge = pl.ds(frame_count, window)
    mine = ext.at[yl, c, body]
    def later(src, dst, device):
        k = MAX_COPIES + len(maybe)
        copy = pltpu.make_async_remote_copy(
            src_ref=src, dst_ref=dst, send_sem=send_sems.at[k], recv_sem=recv_sems.at[k],
            device_id=device, device_id_type=MESH,
        )
        maybe.append(copy)
        return copy

    maybe = []
    first, final = video == 0, video == VIDEO - 1
    lent = later(frames.at[pl.ds(0, window)], ext.at[yl, c, edge], at(before, mp))

    @pl.when(jnp.logical_not(first))
    def _():
        lent.start()

    end_out = [later(frames, mine, outward)]
    mid_out_f = [later(frames, mine, outward)]
    mid_in_f = [later(frames, mine, inward)]
    own_edge = ext.at[yl, c, edge]
    end_out.append(later(own_edge, own_edge, outward))
    mid_out_f.append(later(own_edge, own_edge, outward))
    mid_in_f.append(later(own_edge, own_edge, inward))
    pass_out, pass_mid, pass_far = (
        later(ext.at[line[b], c], ext.at[line[b], c], device)
        for b, device in ((0, outward), (2, inward), (3, inward))
    )

    def frame_start(i):
        @pl.when(is_end)
        def _():
            end_out[i].start()

        @pl.when(is_mid)
        def _():
            mid_in_f[i].start()
            mid_out_f[i].start()

    def frame_pass(i):
        @pl.when(is_mid)
        def _():
            if i == 0:
                for copy in end_out:
                    copy.wait_recv()
                pass_out.start()
                for copy in mid_out_f:
                    copy.wait_recv()
                pass_mid.start()
            else:
                pass_out.wait_recv()
                pass_far.start()

    def b_early(q, i):
        for s in dirs:
            bz[s, 1][i].wait_recv()
            ref = wb.at[q, x, zs[-s % ZS]]
            bz.setdefault((s, 2), []).append(same(ref, to_z[s]))
        for s in dirs:
            ref = wb.at[q, x, zs[-s % ZS]]
            for side in dirs:
                bx.setdefault((side, -s % ZS), []).append(same(ref, to_x[side]))

    b_early(yh, 0)
    frame_start(0)
    pair_b.wait_recv()
    for s in dirs:
        bz[s, 1].append(same(wb.at[other, x, z], to_z[s]))
    pair_a.wait_recv()
    for s in dirs:
        ax[s].append(same(wa.at[other, x, z], to_x[s]))
    for s in dirs:
        bx[s, 0].append(same(wb.at[other, x, z], to_x[s]))

    group = HIGH * XS
    per_shard = shard_rows // out_rows
    half = out_rows // 2
    mixed = group * shard_rows
    to = lax.broadcasted_iota(jnp.int32, (mixed, mixed), 0)
    source = lax.broadcasted_iota(jnp.int32, (mixed, mixed), 1)
    each = 2 * group * per_shard
    inner = to % (group * per_shard)
    wanted = (
        inner // per_shard * shard_rows + inner % per_shard * out_rows
        + to % each // (group * per_shard) * half + to // each
    )
    order_rows[...] = jnp.where(source == wanted, 1.0, 0.0).astype(BF16)

    def sort(z_at):
        block = wa[:, :, z_at, :, size:].reshape(mixed, piece)
        wide[:, z_at] = dot(order_rows[...], block).astype(BF16).reshape(half, each, piece)

    def a_step(step, i):
        for s in dirs:
            z_at = zs[(-s * step) % ZS]
            if step < ZS // 2 - 1:
                ref = wa.at[:, xs[i], z_at]
            else:
                ref = wa.at[0 if s > 0 else 1, xs[i], z_at]
            az[s, step + 1, i] = same(ref, to_z[s])

    own_a.wait()
    a_step(0, 0)

    @pl.when(jnp.logical_not(final))
    def _():
        lent.wait_recv()

    @pl.when(final)
    def _():
        ext[yl, c, frame_count:] = jnp.zeros((window, slab), BF16)

    frame_start(1)

    def b_arrive(step):
        for s in dirs:
            for copy in bz[s, step]:
                copy.wait_recv()
            z_at = zs[(-s * step) % ZS]
            if step < ZS // 2 - 1:
                bz[s, step + 1] = [same(wb.at[:, x, z_at], to_z[s])]
            elif step < ZS // 2:
                bz[s, step + 1] = [same(wb.at[0 if s > 0 else 1, x, z_at], to_z[s])]
        offsets = [-step % ZS, step % ZS] if step < ZS // 2 else [ZS // 2]
        for offset in offsets:
            for s in dirs:
                bx[s, offset] = [same(wb.at[:, x, zs[offset]], to_x[s])]

    bxf = {}

    def b_cross(offset):
        for s in dirs:
            for copy in bx[s, offset]:
                copy.wait_recv()
            ref = wb.at[0 if s > 0 else 1, xs[-s % XS], zs[offset]]
            bxf[s, offset] = same(ref, to_x[s])

    order = (0, 1, 3, 2)

    def a_arrive(step, i):
        for s in dirs:
            az[s, step, i].wait_recv()
        a_step(step, i)

    shared = []
    b_early(other, 1)
    for s in dirs:
        for copy in ax[s]:
            copy.wait_recv()
        axf[s] = same(wa.at[0 if s > 0 else 1, xs[-s % XS], z], to_x[s])
    a_step(0, 1)
    a_step(0, 3)
    frame_pass(0)
    b_arrive(2)
    a_arrive(1, 0)
    for s in dirs:
        axf[s].wait_recv()
    a_step(0, 2)
    b_cross(0)
    sort(z)
    own_b.wait()
    b_arrive(3)
    a_arrive(1, 1)
    b_cross(7)
    a_arrive(1, 3)
    b_arrive(4)
    frame_pass(1)
    b_cross(1)
    a_arrive(1, 2)
    a_arrive(2, 0)
    b_cross(6)
    sort(zs[1])
    sort(zs[-1])
    a_arrive(2, 1)
    b_cross(2)
    a_arrive(2, 3)
    own_frames.wait()

    @pl.when(is_end)
    def _():
        for copy in mid_in_f:
            copy.wait_recv()
        pass_mid.wait_recv()

    for copy in cot_in:
        copy.wait()

    r = lax.broadcasted_iota(jnp.int32, (total, window), 0)
    w = lax.broadcasted_iota(jnp.int32, (total, window), 1)
    put = jnp.concatenate(
        [jnp.where((r - w == starts[j]) & (j < counts[0]), 1.0, 0.0).astype(BF16) for j in range(slots)],
        axis=1,
    )
    direct[...] = dot(put, cot[mp])


    def project_b(i, h):
        u = h * XS + xs[i]
        weights = wb[h, xs[i]].reshape(ZS * shard_rows, qkv_b)
        proj_b[...] += dot(ext[u // CORES, u % CORES], weights)

    for b in range(LOW - 1):
        shared.append(same(ext.at[line[b], c], sibling))
    b_cross(5)
    a_arrive(2, 2)
    sort(zs[2])
    sort(zs[-2])
    b_cross(3)
    a_arrive(3, 0)
    b_cross(4)

    @pl.when(is_end)
    def _():
        pass_far.wait_recv()

    shared.append(same(ext.at[line[LOW - 1], c], sibling))
    proj_a[...] = jnp.zeros_like(proj_a)
    proj_b[...] = jnp.zeros_like(proj_b)
    a_arrive(3, 1)
    for copy in shared:
        copy.wait_recv()
    project_b(0, 0)
    project_b(0, 1)
    a_arrive(3, 3)
    project_b(1, 0)
    a_arrive(3, 2)
    sort(zs[3])
    sort(zs[-3])
    project_b(1, 1)
    project_b(3, 0)
    project_b(3, 1)


    for s in dirs:
        for i in order:
            az[s, ZS // 2, i].wait_recv()
    sort(zs[ZS // 2])

    @pl.loop(0, MP)
    def _(u):
        weights = wa[u // XS, u % XS, :, :, :size].reshape(ZS * shard_rows, size)
        proj_a[...] += dot(ext[u // CORES, u % CORES], weights)

    parts = slab // piece
    acc = jnp.zeros((slots * window, ZS * each), F32)
    for k in range(half):
        block = cot[k // parts, :, (k % parts) * piece:(k % parts + 1) * piece]
        acc += dot(block, wide[k].reshape(ZS * each, piece), NT)
    n = lax.broadcasted_iota(jnp.int32, (ZS * each, ZS * each), 0)
    n_to = lax.broadcasted_iota(jnp.int32, (ZS * each, ZS * each), 1)
    inner = n % (group * per_shard)
    wanted = (
        n % each // (group * per_shard) * size
        + (inner // per_shard * ZS + n // each) * per_shard + inner % per_shard
    )
    columns = jnp.where(n_to == wanted, 1.0, 0.0).astype(BF16)
    heads[...] = dot(acc.astype(BF16), columns).astype(BF16)

    for s in dirs:
        for offset in range(ZS):
            bxf[s, offset].wait_recv()
    for h in range(HIGH):
        project_b(2, h)

    low[:, :qkv_b] = proj_b[...].astype(BF16)
    low[:, qkv_b:] = proj_a[...].astype(BF16)
    rows[...] = dot(put, low[...], TN).astype(BF16)

    for j in range(slots):
        span = slice(j * window, (j + 1) * window)
        for h in range(2):
            base = h * 3 * size
            queries = rows[span, base:base + size]
            keys = rows[span, base + size:base + 2 * size]
            values = rows[span, base + 2 * size:base + 3 * size]
            grad_head = heads[span, h * size:(h + 1) * size]
            scores = dot(queries, keys, NT) * scale
            powers = jnp.exp(scores - jnp.max(scores, axis=-1, keepdims=True))
            attention = powers / jnp.sum(powers, axis=-1, keepdims=True)
            grad_values = dot(attention.astype(BF16), grad_head, TN)
            grad_attention = dot(grad_head, values, NT)
            centre = jnp.sum(attention * grad_attention, axis=-1, keepdims=True)
            grad_scores = (attention * (grad_attention - centre) * scale).astype(BF16)
            grads[span, base:base + size] = dot(grad_scores, keys).astype(BF16)
            grads[span, base + size:base + 2 * size] = dot(grad_scores, queries, TN).astype(BF16)
            grads[span, base + 2 * size:base + 3 * size] = grad_values.astype(BF16)

    placed[...] = dot(put, grads[...]).astype(BF16)

    def group_part(yl_at, c_at):
        u = yl_at * CORES + c_at
        weights_b = wb[u // XS, u % XS].reshape(ZS * shard_rows, qkv_b)
        weights_a = wa[u // XS, u % XS, :, :, :size].reshape(ZS * shard_rows, size)
        return dot(placed[:, :qkv_b], weights_b, NT) + dot(placed[:, qkv_b:], weights_a, NT)

    chunks = (edge, body)
    from_end = [[later(part.at[b, t], near.at[b - 1, t], outward) for b in (1, 2, 3)] for t in chunks]
    from_mid = [[later(part.at[b, t], across.at[3 - b, t], outward) for b in (3, 2)] for t in chunks]
    to_end = [later(part.at[0, t], home.at[t], inward) for t in chunks]

    crossing = {}

    def cross(b):
        give[b] = group_part(line[b], 1 - c).astype(BF16)
        crossing[b] = push(give.at[b], take.at[b], sibling)

    def merge(b):
        own[...] = group_part(line[b], c).astype(BF16).astype(F32)
        crossing[b].wait_recv()
        own[...] += take[b].astype(F32)
        part[b] = own[...].astype(BF16)
        if b < 2:
            @pl.when(is_end if b == 0 else is_mid)
            def _():
                direct[...] += own[...]

    def end_send(*pairs):
        @pl.when(is_end)
        def _():
            for t, b in pairs:
                from_end[t][b - 1].start()

    cross(3)
    cross(2)
    merge(3)
    end_send((0, 3))
    cross(1)
    merge(2)
    end_send((0, 2))
    cross(0)
    merge(1)
    end_send((0, 1), (1, 3), (1, 2), (1, 1))

    def add(ref, t, other_ref):
        ref[...] = (ref[...].astype(F32) + other_ref[...].astype(F32)).astype(BF16)

    def mid_out(t, b):
        from_end[t][b - 1].wait_recv()
        add(part.at[b, chunks[t]], t, near.at[b - 1, chunks[t]])
        from_mid[t][3 - b].start()

    def mid_in(t):
        from_mid[t][0].wait_recv()
        add(part.at[0, chunks[t]], t, across.at[0, chunks[t]])
        to_end[t].start()

    def finish(t):
        @pl.when(is_end)
        def _():
            to_end[t].wait_recv()
            direct[chunks[t]] += home[chunks[t]].astype(F32)

        @pl.when(is_mid)
        def _():
            from_mid[t][1].wait_recv()
            from_end[t][0].wait_recv()
            direct[chunks[t]] += (
                near[0, chunks[t]].astype(F32) + across[1, chunks[t]].astype(F32)
            )

    merge(0)

    @pl.when(is_mid)
    def _():
        mid_out(0, 3)
        mid_out(0, 2)
        mid_in(0)

    finish(0)
    tail[...] = direct[frame_count:].astype(BF16)
    carried = later(tail, tail_in, at(after, mp))

    @pl.when(jnp.logical_not(final))
    def _():
        carried.start()

    @pl.when(is_mid)
    def _():
        mid_out(1, 3)
        mid_in(1)
        mid_out(1, 2)

    finish(1)
    result[...] = direct[:frame_count]

    @pl.when(jnp.logical_not(first))
    def _():
        carried.wait_recv()
        result[:window] += tail_in[...].astype(F32)

    done = pltpu.make_async_copy(result, out, local_sems.at[MAX_LOCAL - 1])
    done.start()
    for copy in copies:
        copy.wait_send()

    @pl.when(jnp.logical_not(first))
    def _():
        lent.wait_send()

    @pl.when(jnp.logical_not(final))
    def _():
        carried.wait_send()

    @pl.when(is_end)
    def _():
        for t in range(2):
            for copy in from_end[t]:
                copy.wait_send()
            end_out[t].wait_send()

    @pl.when(is_mid)
    def _():
        for t in range(2):
            for copy in from_mid[t]:
                copy.wait_send()
            to_end[t].wait_send()
            mid_out_f[t].wait_send()
            mid_in_f[t].wait_send()
        for copy in (pass_out, pass_mid, pass_far):
            copy.wait_send()

    done.wait()


def shards(frames, cotangent, w_qkv, w_out, starts, counts):
    frame_count, slab = frames.shape
    slots, window, width = cotangent.shape
    shard_rows, group, qkv = w_qkv.shape
    size = qkv // 3
    total = frame_count + window
    all_qkv = group * qkv
    qkv_b = all_qkv - size
    out_width = w_out.shape[0] * group * width // shard_rows
    out_rows = group * width // out_width
    smem = pl.BlockSpec(memory_space=pltpu.SMEM)
    hbm = pl.BlockSpec(memory_space=pl.ANY)
    vmem = pltpu.VMEM
    return pl.pallas_call(
        kernel,
        out_shape=jax.ShapeDtypeStruct((frame_count, slab), F32),
        in_specs=[smem, smem, hbm, hbm, pl.BlockSpec(memory_space=vmem), pl.BlockSpec(memory_space=vmem)],
        out_specs=hbm,
        scratch_shapes=[
            vmem((shard_rows, size + out_width), BF16),
            vmem((shard_rows, qkv_b), BF16),
            vmem((shard_rows, out_width), F32),
            vmem((HIGH, XS, ZS, shard_rows, size + out_width), BF16),
            vmem((HIGH, XS, ZS, shard_rows, qkv_b), BF16),
            vmem((LOW, CORES, total, slab), BF16),
            vmem((MP, slots * window, slab), BF16),
            vmem((out_rows // 2, ZS, 2 * HIGH * XS * shard_rows // out_rows, out_width), BF16),
            vmem((HIGH * XS * shard_rows, HIGH * XS * shard_rows), BF16),
            vmem((total, size), F32),
            vmem((total, qkv_b), F32),
            vmem((total, all_qkv), BF16),
            vmem((slots * window, all_qkv), BF16),
            vmem((slots * window, group * size), BF16),
            vmem((slots * window, all_qkv), BF16),
            vmem((total, all_qkv), BF16),
            vmem((total, slab), F32),
            vmem((total, slab), F32),
            vmem((LOW, total, slab), BF16),
            vmem((LOW, total, slab), BF16),
            vmem((LOW, total, slab), BF16),
            vmem((LOW - 1, total, slab), BF16),
            vmem((2, total, slab), BF16),
            vmem((total, slab), BF16),
            vmem((window, slab), BF16),
            vmem((window, slab), BF16),
            vmem((frame_count, slab), F32),
            pltpu.SemaphoreType.DMA((MAX_COPIES + MAX_MAYBE,)),
            pltpu.SemaphoreType.DMA((MAX_COPIES + MAX_MAYBE,)),
            pltpu.SemaphoreType.DMA((MAX_LOCAL,)),
        ],
        compiler_params=pltpu.CompilerParams(
            collective_id=0, has_side_effects=True, vmem_limit_bytes=56 * 2**20
        ),
    )(starts, counts, frames, cotangent.reshape(slots * window, width), w_qkv, w_out)


def solution(mesh):
    placed = (
        P("video", "mp"),
        P("video", None, None),
        P("video", "mp", None),
        P("video", "mp", None),
        P("video"),
        P("video"),
    )
    return jax.shard_map(
        shards, mesh=mesh, in_specs=placed, out_specs=P("video", "mp"), check_vma=False
    )
```

```python
import math

import jax
import jax.numpy as jnp
from jax import lax
from jax.experimental import pallas as pl
from jax.experimental.pallas import tpu as pltpu
from jax.sharding import PartitionSpec as P

HIGH, XS, ZS, LOW, CORES = 2, 4, 8, 4, 2
VIDEO = HIGH * XS * ZS
MP = LOW * CORES
MAX_COPIES = 128
MAX_MAYBE = 32
MAX_LOCAL = 16
MESH = pl.DeviceIdType.MESH
NT = (((1,), (1,)), ((), ()))
TN = (((0,), (0,)), ((), ()))
F32, BF16 = jnp.float32, jnp.bfloat16


def dot(a, b, dims=(((1,), (0,)), ((), ()))):
    return lax.dot_general(a, b, dims, preferred_element_type=F32)


def kernel(
    starts, counts, frames, cotangent, w_qkv, w_out, out,
    first_shard, second_shard, lines, wa, wb, ext, cot, wide, order_rows, proj_a, proj_b, low, rows, heads, grads, placed,
    direct, own, give, take, part, near, across, home, tail, tail_in, result,
    send_sems, recv_sems, local_sems,
):
    slots = starts.shape[0]
    frame_count, slab = frames.shape
    window = ext.shape[2] - frame_count
    total = ext.shape[2]
    shard_rows = w_qkv.shape[0]
    size = proj_a.shape[1]
    qkv_b = proj_b.shape[1]
    piece = wa.shape[4] - size
    out_rows = 2 * wide.shape[0]
    scale = 1.0 / math.sqrt(size)

    video, mp = lax.axis_index("video"), lax.axis_index("mp")
    yh, x, z = video // (XS * ZS), (video // ZS) % XS, video % ZS
    yl, c = mp // CORES, mp % CORES
    other = 1 - yh
    xs = [(x + i) % XS for i in range(XS)]
    zs = [(z + i) % ZS for i in range(ZS)]
    yls = [(yl + i) % LOW for i in range(LOW)]
    before, after = (video + VIDEO - 1) % VIDEO, (video + 1) % VIDEO

    def at(video_at, mp_at):
        return {"video": video_at, "mp": mp_at}

    def place(yh_at, x_at, z_at):
        return (yh_at * XS + x_at) * ZS + z_at

    partner = at(place(other, x, z), mp)
    to_x = {1: at(place(yh, xs[1], z), mp), -1: at(place(yh, xs[-1], z), mp)}
    to_z = {1: at(place(yh, x, zs[1]), mp), -1: at(place(yh, x, zs[-1]), mp)}
    sibling = at(video, yl * CORES + 1 - c)

    last = LOW - 1
    lower = yl < LOW // 2
    line = [jnp.where(lower, b, last - b) for b in range(LOW)]
    is_end = (yl == 0) | (yl == last)
    is_mid = jnp.logical_not(is_end)
    outward = at(video, jnp.where(lower, yl + 1, yl - 1) * CORES + c)
    inward = at(video, jnp.where(lower, yl + last, yl + 1) % LOW * CORES + c)

    met = [partner, to_x[1], to_x[-1], to_z[1], to_z[-1], sibling]
    met += [at(video, yls[d] * CORES + c) for d in range(1, LOW)]
    met += [at(before, mp), at(after, mp)]
    barrier = pltpu.get_barrier_semaphore()
    for device in met:
        pl.semaphore_signal(barrier, inc=1, device_id=device, device_id_type=MESH)

    locals_ = []

    def stage(src, dst):
        copy = pltpu.make_async_copy(src, dst, local_sems.at[len(locals_)])
        copy.start()
        locals_.append(copy)
        return copy

    own_frames = stage(frames, ext.at[yl, c, pl.ds(0, frame_count)])
    cot_in = [stage(cotangent.at[:, pl.ds(u * slab, slab)], cot.at[u]) for u in range(MP)]

    qkv = w_qkv[...].astype(F32)
    panels = w_out[...].astype(F32)
    head_qkv = 3 * size
    second_shard[:, :head_qkv] = qkv[:, 0].astype(BF16)
    second_shard[:, head_qkv:] = qkv[:, 1, :qkv_b - head_qkv].astype(BF16)
    first_shard[:, :size] = qkv[:, 1, qkv_b - head_qkv:].astype(BF16)
    for e in range(panels.shape[0]):
        for h in range(2):
            for k in range(out_rows // 2):
                row = (e * 2 + h) * (out_rows // 2) + k
                lines[row:row + 1] = panels[e, h:h + 1, k * piece:(k + 1) * piece]
    first_shard[:, size:] = lines[...].astype(BF16)
    own_a = stage(first_shard, wa.at[yh, x, z])
    own_b = stage(second_shard, wb.at[yh, x, z])

    pl.semaphore_wait(barrier, len(met))

    copies = []

    def push(src, dst, device):
        k = len(copies)
        copy = pltpu.make_async_remote_copy(
            src_ref=src, dst_ref=dst, send_sem=send_sems.at[k], recv_sem=recv_sems.at[k],
            device_id=device, device_id_type=MESH,
        )
        copy.start()
        copies.append(copy)
        return copy

    def same(ref, device):
        return push(ref, ref, device)

    dirs = (1, -1)

    pair_b = push(second_shard, wb.at[yh, x, z], partner)
    pair_a = push(first_shard, wa.at[yh, x, z], partner)
    bz, bx, az, ax, axf = {}, {}, {}, {}, {}
    for s in dirs:
        bz[s, 1] = [push(second_shard, wb.at[yh, x, z], to_z[s])]
    for s in dirs:
        ax[s] = [push(first_shard, wa.at[yh, x, z], to_x[s])]
    for s in dirs:
        bx[s, 0] = [push(second_shard, wb.at[yh, x, z], to_x[s])]

    body = pl.ds(0, frame_count)
    edge = pl.ds(frame_count, window)
    mine = ext.at[yl, c, body]
    def later(src, dst, device):
        k = MAX_COPIES + len(maybe)
        copy = pltpu.make_async_remote_copy(
            src_ref=src, dst_ref=dst, send_sem=send_sems.at[k], recv_sem=recv_sems.at[k],
            device_id=device, device_id_type=MESH,
        )
        maybe.append(copy)
        return copy

    maybe = []
    first, final = video == 0, video == VIDEO - 1
    lent = later(frames.at[pl.ds(0, window)], ext.at[yl, c, edge], at(before, mp))

    @pl.when(jnp.logical_not(first))
    def _():
        lent.start()

    end_out = [later(frames, mine, outward)]
    mid_out_f = [later(frames, mine, outward)]
    mid_in_f = [later(frames, mine, inward)]
    own_edge = ext.at[yl, c, edge]
    end_out.append(later(own_edge, own_edge, outward))
    mid_out_f.append(later(own_edge, own_edge, outward))
    mid_in_f.append(later(own_edge, own_edge, inward))
    pass_out, pass_mid, pass_far = (
        later(ext.at[line[b], c], ext.at[line[b], c], device)
        for b, device in ((0, outward), (2, inward), (3, inward))
    )

    def frame_start(i):
        @pl.when(is_end)
        def _():
            end_out[i].start()

        @pl.when(is_mid)
        def _():
            mid_in_f[i].start()
            mid_out_f[i].start()

    def frame_pass(i):
        @pl.when(is_mid)
        def _():
            if i == 0:
                for copy in end_out:
                    copy.wait_recv()
                pass_out.start()
                for copy in mid_out_f:
                    copy.wait_recv()
                pass_mid.start()
            else:
                pass_out.wait_recv()
                pass_far.start()

    def b_early(q, i):
        for s in dirs:
            bz[s, 1][i].wait_recv()
            ref = wb.at[q, x, zs[-s % ZS]]
            bz.setdefault((s, 2), []).append(same(ref, to_z[s]))
        for s in dirs:
            ref = wb.at[q, x, zs[-s % ZS]]
            for side in dirs:
                bx.setdefault((side, -s % ZS), []).append(same(ref, to_x[side]))

    b_early(yh, 0)
    frame_start(0)
    pair_b.wait_recv()
    for s in dirs:
        bz[s, 1].append(same(wb.at[other, x, z], to_z[s]))
    pair_a.wait_recv()
    for s in dirs:
        ax[s].append(same(wa.at[other, x, z], to_x[s]))
    for s in dirs:
        bx[s, 0].append(same(wb.at[other, x, z], to_x[s]))

    group = HIGH * XS
    per_shard = shard_rows // out_rows
    half = out_rows // 2
    mixed = group * shard_rows
    each = 2 * group * per_shard

    def make_order():
        to = lax.broadcasted_iota(jnp.int32, (mixed, 1), 0)
        inner = to % (group * per_shard)
        wanted = (
            inner // per_shard * shard_rows + inner % per_shard * out_rows
            + to % each // (group * per_shard) * half + to // each
        )
        source = lax.broadcasted_iota(jnp.int32, (mixed, mixed), 1)
        order_rows[...] = jnp.where(source == wanted, 1.0, 0.0).astype(BF16)

    def sort(z_at):
        block = wa[:, :, z_at, :, size:].reshape(mixed, piece)
        wide[:, z_at] = dot(order_rows[...], block).astype(BF16).reshape(half, each, piece)

    def a_step(step, i):
        for s in dirs:
            z_at = zs[(-s * step) % ZS]
            if step < ZS // 2 - 1:
                ref = wa.at[:, xs[i], z_at]
            else:
                ref = wa.at[0 if s > 0 else 1, xs[i], z_at]
            az[s, step + 1, i] = same(ref, to_z[s])

    own_a.wait()
    a_step(0, 0)

    @pl.when(jnp.logical_not(final))
    def _():
        lent.wait_recv()

    @pl.when(final)
    def _():
        ext[yl, c, frame_count:] = jnp.zeros((window, slab), BF16)

    frame_start(1)

    def b_arrive(step):
        for s in dirs:
            for copy in bz[s, step]:
                copy.wait_recv()
            z_at = zs[(-s * step) % ZS]
            if step < ZS // 2 - 1:
                bz[s, step + 1] = [same(wb.at[:, x, z_at], to_z[s])]
            elif step < ZS // 2:
                bz[s, step + 1] = [same(wb.at[0 if s > 0 else 1, x, z_at], to_z[s])]
        offsets = [-step % ZS, step % ZS] if step < ZS // 2 else [ZS // 2]
        for offset in offsets:
            for s in dirs:
                bx[s, offset] = [same(wb.at[:, x, zs[offset]], to_x[s])]

    bxf = {}

    def b_cross(offset):
        for s in dirs:
            for copy in bx[s, offset]:
                copy.wait_recv()
            ref = wb.at[0 if s > 0 else 1, xs[-s % XS], zs[offset]]
            bxf[s, offset] = same(ref, to_x[s])

    order = (0, 1, 3, 2)

    def a_arrive(step, i):
        for s in dirs:
            az[s, step, i].wait_recv()
        a_step(step, i)

    shared = []
    b_early(other, 1)
    for s in dirs:
        for copy in ax[s]:
            copy.wait_recv()
        axf[s] = same(wa.at[0 if s > 0 else 1, xs[-s % XS], z], to_x[s])
    a_step(0, 1)
    a_step(0, 3)
    frame_pass(0)
    b_arrive(2)
    a_arrive(1, 0)
    for s in dirs:
        axf[s].wait_recv()
    a_step(0, 2)
    b_cross(0)
    make_order()
    sort(z)
    own_b.wait()
    b_arrive(3)
    a_arrive(1, 1)
    b_cross(7)
    a_arrive(1, 3)
    b_arrive(4)
    frame_pass(1)
    b_cross(1)
    a_arrive(1, 2)
    a_arrive(2, 0)
    b_cross(6)
    sort(zs[1])
    sort(zs[-1])
    a_arrive(2, 1)
    b_cross(2)
    a_arrive(2, 3)
    own_frames.wait()

    @pl.when(is_end)
    def _():
        for copy in mid_in_f:
            copy.wait_recv()
        pass_mid.wait_recv()

    for copy in cot_in:
        copy.wait()

    r = lax.broadcasted_iota(jnp.int32, (total, window), 0)
    w = lax.broadcasted_iota(jnp.int32, (total, window), 1)
    put = jnp.concatenate(
        [jnp.where((r - w == starts[j]) & (j < counts[0]), 1.0, 0.0).astype(BF16) for j in range(slots)],
        axis=1,
    )
    direct[...] = dot(put, cot[mp])


    def project_b(i, h):
        u = h * XS + xs[i]
        weights = wb[h, xs[i]].reshape(ZS * shard_rows, qkv_b)
        proj_b[...] += dot(ext[u // CORES, u % CORES], weights)

    for b in range(LOW - 1):
        shared.append(same(ext.at[line[b], c], sibling))
    b_cross(5)
    a_arrive(2, 2)
    sort(zs[2])
    sort(zs[-2])
    b_cross(3)
    a_arrive(3, 0)
    b_cross(4)

    @pl.when(is_end)
    def _():
        pass_far.wait_recv()

    shared.append(same(ext.at[line[LOW - 1], c], sibling))
    proj_a[...] = jnp.zeros_like(proj_a)
    proj_b[...] = jnp.zeros_like(proj_b)
    a_arrive(3, 1)
    for copy in shared:
        copy.wait_recv()
    project_b(0, 0)
    project_b(0, 1)
    a_arrive(3, 3)
    project_b(1, 0)
    a_arrive(3, 2)
    sort(zs[3])
    sort(zs[-3])
    project_b(1, 1)
    project_b(3, 0)
    project_b(3, 1)


    for s in dirs:
        for i in order:
            az[s, ZS // 2, i].wait_recv()
    sort(zs[ZS // 2])

    @pl.loop(0, MP)
    def _(u):
        weights = wa[u // XS, u % XS, :, :, :size].reshape(ZS * shard_rows, size)
        proj_a[...] += dot(ext[u // CORES, u % CORES], weights)

    parts = slab // piece
    acc = jnp.zeros((slots * window, ZS * each), F32)
    for k in range(half):
        block = cot[k // parts, :, (k % parts) * piece:(k % parts + 1) * piece]
        acc += dot(block, wide[k].reshape(ZS * each, piece), NT)
    n = lax.broadcasted_iota(jnp.int32, (ZS * each, 1), 0)
    n_to = lax.broadcasted_iota(jnp.int32, (ZS * each, ZS * each), 1)
    inner = n % (group * per_shard)
    wanted = (
        n % each // (group * per_shard) * size
        + (inner // per_shard * ZS + n // each) * per_shard + inner % per_shard
    )
    columns = jnp.where(n_to == wanted, 1.0, 0.0).astype(BF16)
    heads[...] = dot(acc.astype(BF16), columns).astype(BF16)

    for s in dirs:
        for offset in range(ZS):
            bxf[s, offset].wait_recv()
    for h in range(HIGH):
        project_b(2, h)

    low[:, :qkv_b] = proj_b[...].astype(BF16)
    low[:, qkv_b:] = proj_a[...].astype(BF16)
    rows[...] = dot(put, low[...], TN).astype(BF16)

    for j in range(slots):
        span = slice(j * window, (j + 1) * window)
        for h in range(2):
            base = h * 3 * size
            queries = rows[span, base:base + size]
            keys = rows[span, base + size:base + 2 * size]
            values = rows[span, base + 2 * size:base + 3 * size]
            grad_head = heads[span, h * size:(h + 1) * size]
            scores = dot(queries, keys, NT) * scale
            powers = jnp.exp(scores - jnp.max(scores, axis=-1, keepdims=True))
            attention = powers / jnp.sum(powers, axis=-1, keepdims=True)
            grad_values = dot(attention.astype(BF16), grad_head, TN)
            grad_attention = dot(grad_head, values, NT)
            centre = jnp.sum(attention * grad_attention, axis=-1, keepdims=True)
            grad_scores = (attention * (grad_attention - centre) * scale).astype(BF16)
            grads[span, base:base + size] = dot(grad_scores, keys).astype(BF16)
            grads[span, base + size:base + 2 * size] = dot(grad_scores, queries, TN).astype(BF16)
            grads[span, base + 2 * size:base + 3 * size] = grad_values.astype(BF16)

    placed[...] = dot(put, grads[...]).astype(BF16)

    def group_part(yl_at, c_at):
        u = yl_at * CORES + c_at
        weights_b = wb[u // XS, u % XS].reshape(ZS * shard_rows, qkv_b)
        weights_a = wa[u // XS, u % XS, :, :, :size].reshape(ZS * shard_rows, size)
        return dot(placed[...], jnp.concatenate([weights_b, weights_a], axis=1), NT)

    chunks = (edge, body)
    from_end = [[later(part.at[b, t], near.at[b - 1, t], outward) for b in (1, 2, 3)] for t in chunks]
    from_mid = [[later(part.at[b, t], across.at[3 - b, t], outward) for b in (3, 2)] for t in chunks]
    to_end = [later(part.at[0, t], home.at[t], inward) for t in chunks]

    crossing = {}

    def cross(b):
        give[b] = group_part(line[b], 1 - c).astype(BF16)
        crossing[b] = push(give.at[b], take.at[b], sibling)

    def merge(b):
        own[...] = group_part(line[b], c).astype(BF16).astype(F32)
        crossing[b].wait_recv()
        own[...] += take[b].astype(F32)
        part[b] = own[...].astype(BF16)
        if b < 2:
            @pl.when(is_end if b == 0 else is_mid)
            def _():
                direct[...] += own[...]

    def end_send(*pairs):
        @pl.when(is_end)
        def _():
            for t, b in pairs:
                from_end[t][b - 1].start()

    cross(3)
    cross(2)
    merge(3)
    end_send((0, 3))
    cross(1)
    merge(2)
    end_send((0, 2))
    cross(0)
    merge(1)
    end_send((0, 1), (1, 3), (1, 2), (1, 1))

    def add(ref, t, other_ref):
        ref[...] = (ref[...].astype(F32) + other_ref[...].astype(F32)).astype(BF16)

    def mid_out(t, b):
        from_end[t][b - 1].wait_recv()
        add(part.at[b, chunks[t]], t, near.at[b - 1, chunks[t]])
        from_mid[t][3 - b].start()

    def mid_in(t):
        from_mid[t][0].wait_recv()
        add(part.at[0, chunks[t]], t, across.at[0, chunks[t]])
        to_end[t].start()

    def finish(t):
        @pl.when(is_end)
        def _():
            to_end[t].wait_recv()
            direct[chunks[t]] += home[chunks[t]].astype(F32)

        @pl.when(is_mid)
        def _():
            from_mid[t][1].wait_recv()
            from_end[t][0].wait_recv()
            direct[chunks[t]] += (
                near[0, chunks[t]].astype(F32) + across[1, chunks[t]].astype(F32)
            )

    merge(0)

    @pl.when(is_mid)
    def _():
        mid_out(0, 3)
        mid_out(0, 2)
        mid_in(0)

    finish(0)
    tail[...] = direct[frame_count:].astype(BF16)
    carried = later(tail, tail_in, at(after, mp))

    @pl.when(jnp.logical_not(final))
    def _():
        carried.start()

    @pl.when(is_mid)
    def _():
        mid_out(1, 3)
        mid_in(1)
        mid_out(1, 2)

    for copy in copies:
        copy.wait_send()

    @pl.when(jnp.logical_not(first))
    def _():
        lent.wait_send()

    @pl.when(is_end)
    def _():
        for copy in end_out:
            copy.wait_send()

    @pl.when(is_mid)
    def _():
        for copy in (*mid_out_f, *mid_in_f, pass_out, pass_mid, pass_far):
            copy.wait_send()

    finish(1)
    result[...] = direct[:frame_count]

    @pl.when(jnp.logical_not(first))
    def _():
        carried.wait_recv()
        result[:window] += tail_in[...].astype(F32)

    done = pltpu.make_async_copy(result, out, local_sems.at[MAX_LOCAL - 1])
    done.start()
    @pl.when(jnp.logical_not(final))
    def _():
        carried.wait_send()

    @pl.when(is_end)
    def _():
        for t in range(2):
            for copy in from_end[t]:
                copy.wait_send()

    @pl.when(is_mid)
    def _():
        for t in range(2):
            for copy in from_mid[t]:
                copy.wait_send()
            to_end[t].wait_send()

    done.wait()


def shards(frames, cotangent, w_qkv, w_out, starts, counts):
    frame_count, slab = frames.shape
    slots, window, width = cotangent.shape
    shard_rows, group, qkv = w_qkv.shape
    size = qkv // 3
    total = frame_count + window
    all_qkv = group * qkv
    qkv_b = all_qkv - size
    out_width = w_out.shape[0] * group * width // shard_rows
    out_rows = group * width // out_width
    smem = pl.BlockSpec(memory_space=pltpu.SMEM)
    hbm = pl.BlockSpec(memory_space=pl.ANY)
    vmem = pltpu.VMEM
    return pl.pallas_call(
        kernel,
        out_shape=jax.ShapeDtypeStruct((frame_count, slab), F32),
        in_specs=[smem, smem, hbm, hbm, pl.BlockSpec(memory_space=vmem), pl.BlockSpec(memory_space=vmem)],
        out_specs=hbm,
        scratch_shapes=[
            vmem((shard_rows, size + out_width), BF16),
            vmem((shard_rows, qkv_b), BF16),
            vmem((shard_rows, out_width), F32),
            vmem((HIGH, XS, ZS, shard_rows, size + out_width), BF16),
            vmem((HIGH, XS, ZS, shard_rows, qkv_b), BF16),
            vmem((LOW, CORES, total, slab), BF16),
            vmem((MP, slots * window, slab), BF16),
            vmem((out_rows // 2, ZS, 2 * HIGH * XS * shard_rows // out_rows, out_width), BF16),
            vmem((HIGH * XS * shard_rows, HIGH * XS * shard_rows), BF16),
            vmem((total, size), F32),
            vmem((total, qkv_b), F32),
            vmem((total, all_qkv), BF16),
            vmem((slots * window, all_qkv), BF16),
            vmem((slots * window, group * size), BF16),
            vmem((slots * window, all_qkv), BF16),
            vmem((total, all_qkv), BF16),
            vmem((total, slab), F32),
            vmem((total, slab), F32),
            vmem((LOW, total, slab), BF16),
            vmem((LOW, total, slab), BF16),
            vmem((LOW, total, slab), BF16),
            vmem((LOW - 1, total, slab), BF16),
            vmem((2, total, slab), BF16),
            vmem((total, slab), BF16),
            vmem((window, slab), BF16),
            vmem((window, slab), BF16),
            vmem((frame_count, slab), F32),
            pltpu.SemaphoreType.DMA((MAX_COPIES + MAX_MAYBE,)),
            pltpu.SemaphoreType.DMA((MAX_COPIES + MAX_MAYBE,)),
            pltpu.SemaphoreType.DMA((MAX_LOCAL,)),
        ],
        compiler_params=pltpu.CompilerParams(
            collective_id=0, has_side_effects=True, vmem_limit_bytes=56 * 2**20
        ),
    )(starts, counts, frames, cotangent.reshape(slots * window, width), w_qkv, w_out)


def solution(mesh):
    placed = (
        P("video", "mp"),
        P("video", None, None),
        P("video", "mp", None),
        P("video", "mp", None),
        P("video"),
        P("video"),
    )
    return jax.shard_map(
        shards, mesh=mesh, in_specs=placed, out_specs=P("video", "mp"), check_vma=False
    )
```

```python
import math

import jax
import jax.numpy as jnp
from jax import lax
from jax.experimental import pallas as pl
from jax.experimental.pallas import tpu as pltpu
from jax.sharding import PartitionSpec as P

HIGH, XS, ZS, LOW, CORES = 2, 4, 8, 4, 2
VIDEO = HIGH * XS * ZS
MP = LOW * CORES
MAX_COPIES = 128
MAX_MAYBE = 32
MAX_LOCAL = 16
MESH = pl.DeviceIdType.MESH
NT = (((1,), (1,)), ((), ()))
TN = (((0,), (0,)), ((), ()))
F32, BF16 = jnp.float32, jnp.bfloat16


def dot(a, b, dims=(((1,), (0,)), ((), ()))):
    return lax.dot_general(a, b, dims, preferred_element_type=F32)


def kernel(
    starts, counts, frames, cotangent, w_qkv, w_out, out,
    first_shard, second_shard, lines, wa, wb, ext, cot, wide, order_rows, proj_a, proj_b, low, rows, heads, grads, placed,
    direct, own, give, take, part, near, across, home, tail, tail_in, result,
    send_sems, recv_sems, local_sems,
):
    slots = starts.shape[0]
    frame_count, slab = frames.shape
    window = ext.shape[2] - frame_count
    total = ext.shape[2]
    shard_rows = w_qkv.shape[0]
    size = proj_a.shape[1]
    qkv_b = proj_b.shape[1]
    piece = wa.shape[4] - size
    out_rows = 2 * wide.shape[0]
    scale = 1.0 / math.sqrt(size)

    video, mp = lax.axis_index("video"), lax.axis_index("mp")
    yh, x, z = video // (XS * ZS), (video // ZS) % XS, video % ZS
    yl, c = mp // CORES, mp % CORES
    other = 1 - yh
    xs = [(x + i) % XS for i in range(XS)]
    zs = [(z + i) % ZS for i in range(ZS)]
    yls = [(yl + i) % LOW for i in range(LOW)]
    before, after = (video + VIDEO - 1) % VIDEO, (video + 1) % VIDEO

    def at(video_at, mp_at):
        return {"video": video_at, "mp": mp_at}

    def place(yh_at, x_at, z_at):
        return (yh_at * XS + x_at) * ZS + z_at

    partner = at(place(other, x, z), mp)
    to_x = {1: at(place(yh, xs[1], z), mp), -1: at(place(yh, xs[-1], z), mp)}
    to_z = {1: at(place(yh, x, zs[1]), mp), -1: at(place(yh, x, zs[-1]), mp)}
    sibling = at(video, yl * CORES + 1 - c)

    last = LOW - 1
    lower = yl < LOW // 2
    line = [jnp.where(lower, b, last - b) for b in range(LOW)]
    is_end = (yl == 0) | (yl == last)
    is_mid = jnp.logical_not(is_end)
    outward = at(video, jnp.where(lower, yl + 1, yl - 1) * CORES + c)
    inward = at(video, jnp.where(lower, yl + last, yl + 1) % LOW * CORES + c)

    met = [partner, to_x[1], to_x[-1], to_z[1], to_z[-1], sibling]
    met += [at(video, yls[d] * CORES + c) for d in range(1, LOW)]
    met += [at(before, mp), at(after, mp)]
    barrier = pltpu.get_barrier_semaphore()
    for device in met:
        pl.semaphore_signal(barrier, inc=1, device_id=device, device_id_type=MESH)

    locals_ = []

    def stage(src, dst):
        copy = pltpu.make_async_copy(src, dst, local_sems.at[len(locals_)])
        copy.start()
        locals_.append(copy)
        return copy

    own_frames = stage(frames, ext.at[yl, c, pl.ds(0, frame_count)])
    cot_in = [stage(cotangent.at[:, pl.ds(u * slab, slab)], cot.at[u]) for u in range(MP)]

    qkv = w_qkv[...].astype(F32)
    panels = w_out[...].astype(F32)
    head_qkv = 3 * size
    second_shard[:, :head_qkv] = qkv[:, 0].astype(BF16)
    second_shard[:, head_qkv:] = qkv[:, 1, :qkv_b - head_qkv].astype(BF16)
    first_shard[:, :size] = qkv[:, 1, qkv_b - head_qkv:].astype(BF16)
    for e in range(panels.shape[0]):
        for h in range(2):
            for k in range(out_rows // 2):
                row = (e * 2 + h) * (out_rows // 2) + k
                lines[row:row + 1] = panels[e, h:h + 1, k * piece:(k + 1) * piece]
    first_shard[:, size:] = lines[...].astype(BF16)
    own_a = stage(first_shard, wa.at[yh, x, z])
    own_b = stage(second_shard, wb.at[yh, x, z])

    pl.semaphore_wait(barrier, len(met))

    copies = []

    def push(src, dst, device):
        k = len(copies)
        copy = pltpu.make_async_remote_copy(
            src_ref=src, dst_ref=dst, send_sem=send_sems.at[k], recv_sem=recv_sems.at[k],
            device_id=device, device_id_type=MESH,
        )
        copy.start()
        copies.append(copy)
        return copy

    def same(ref, device):
        return push(ref, ref, device)

    dirs = (1, -1)

    pair_b = push(second_shard, wb.at[yh, x, z], partner)
    pair_a = push(first_shard, wa.at[yh, x, z], partner)
    bz, bx, az, ax, axf = {}, {}, {}, {}, {}
    for s in dirs:
        bz[s, 1] = [push(second_shard, wb.at[yh, x, z], to_z[s])]
    for s in dirs:
        ax[s] = [push(first_shard, wa.at[yh, x, z], to_x[s])]
    for s in dirs:
        bx[s, 0] = [push(second_shard, wb.at[yh, x, z], to_x[s])]

    body = pl.ds(0, frame_count)
    edge = pl.ds(frame_count, window)
    mine = ext.at[yl, c, body]
    def later(src, dst, device):
        k = MAX_COPIES + len(maybe)
        copy = pltpu.make_async_remote_copy(
            src_ref=src, dst_ref=dst, send_sem=send_sems.at[k], recv_sem=recv_sems.at[k],
            device_id=device, device_id_type=MESH,
        )
        maybe.append(copy)
        return copy

    maybe = []
    first, final = video == 0, video == VIDEO - 1
    lent = later(frames.at[pl.ds(0, window)], ext.at[yl, c, edge], at(before, mp))

    @pl.when(jnp.logical_not(first))
    def _():
        lent.start()

    end_out = [later(frames, mine, outward)]
    mid_out_f = [later(frames, mine, outward)]
    mid_in_f = [later(frames, mine, inward)]
    own_edge = ext.at[yl, c, edge]
    end_out.append(later(own_edge, own_edge, outward))
    mid_out_f.append(later(own_edge, own_edge, outward))
    mid_in_f.append(later(own_edge, own_edge, inward))
    pass_out, pass_mid, pass_far = (
        later(ext.at[line[b], c], ext.at[line[b], c], device)
        for b, device in ((0, outward), (2, inward), (3, inward))
    )

    def frame_start(i):
        @pl.when(is_end)
        def _():
            end_out[i].start()

        @pl.when(is_mid)
        def _():
            mid_in_f[i].start()
            mid_out_f[i].start()

    def frame_pass(i):
        @pl.when(is_mid)
        def _():
            if i == 0:
                for copy in end_out:
                    copy.wait_recv()
                pass_out.start()
                for copy in mid_out_f:
                    copy.wait_recv()
                pass_mid.start()
            else:
                pass_out.wait_recv()
                pass_far.start()

    def b_early(q, i):
        for s in dirs:
            bz[s, 1][i].wait_recv()
            ref = wb.at[q, x, zs[-s % ZS]]
            bz.setdefault((s, 2), []).append(same(ref, to_z[s]))
        for s in dirs:
            ref = wb.at[q, x, zs[-s % ZS]]
            for side in dirs:
                bx.setdefault((side, -s % ZS), []).append(same(ref, to_x[side]))

    b_early(yh, 0)
    frame_start(0)
    pair_b.wait_recv()
    for s in dirs:
        bz[s, 1].append(same(wb.at[other, x, z], to_z[s]))
    pair_a.wait_recv()
    for s in dirs:
        ax[s].append(same(wa.at[other, x, z], to_x[s]))
    for s in dirs:
        bx[s, 0].append(same(wb.at[other, x, z], to_x[s]))

    group = HIGH * XS
    per_shard = shard_rows // out_rows
    half = out_rows // 2
    mixed = group * shard_rows
    each = 2 * group * per_shard

    def make_order():
        to = lax.broadcasted_iota(jnp.int32, (mixed, 1), 0)
        inner = to % (group * per_shard)
        wanted = (
            inner // per_shard * shard_rows + inner % per_shard * out_rows
            + to % each // (group * per_shard) * half + to // each
        )
        source = lax.broadcasted_iota(jnp.int32, (mixed, mixed), 1)
        order_rows[...] = jnp.where(source == wanted, 1.0, 0.0).astype(BF16)

    def sort(z_at):
        block = wa[:, :, z_at, :, size:].reshape(mixed, piece)
        wide[:, z_at] = dot(order_rows[...], block).astype(BF16).reshape(half, each, piece)

    def a_step(step, i):
        for s in dirs:
            z_at = zs[(-s * step) % ZS]
            if step < ZS // 2 - 1:
                ref = wa.at[:, xs[i], z_at]
            else:
                ref = wa.at[0 if s > 0 else 1, xs[i], z_at]
            az[s, step + 1, i] = same(ref, to_z[s])

    own_a.wait()
    a_step(0, 0)

    @pl.when(jnp.logical_not(final))
    def _():
        lent.wait_recv()

    @pl.when(final)
    def _():
        ext[yl, c, frame_count:] = jnp.zeros((window, slab), BF16)

    frame_start(1)

    def b_arrive(step):
        for s in dirs:
            for copy in bz[s, step]:
                copy.wait_recv()
            z_at = zs[(-s * step) % ZS]
            if step < ZS // 2 - 1:
                bz[s, step + 1] = [same(wb.at[:, x, z_at], to_z[s])]
            elif step < ZS // 2:
                bz[s, step + 1] = [same(wb.at[0 if s > 0 else 1, x, z_at], to_z[s])]
        offsets = [-step % ZS, step % ZS] if step < ZS // 2 else [ZS // 2]
        for offset in offsets:
            for s in dirs:
                bx[s, offset] = [same(wb.at[:, x, zs[offset]], to_x[s])]

    bxf = {}

    def b_cross(offset):
        for s in dirs:
            for copy in bx[s, offset]:
                copy.wait_recv()
            ref = wb.at[0 if s > 0 else 1, xs[-s % XS], zs[offset]]
            bxf[s, offset] = same(ref, to_x[s])

    order = (0, 1, 3, 2)

    def a_arrive(step, i):
        for s in dirs:
            az[s, step, i].wait_recv()
        a_step(step, i)

    shared = []
    b_early(other, 1)
    for s in dirs:
        for copy in ax[s]:
            copy.wait_recv()
        axf[s] = same(wa.at[0 if s > 0 else 1, xs[-s % XS], z], to_x[s])
    a_step(0, 1)
    a_step(0, 3)
    frame_pass(0)
    b_arrive(2)
    a_arrive(1, 0)
    for s in dirs:
        axf[s].wait_recv()
    a_step(0, 2)
    b_cross(0)
    make_order()
    sort(z)
    own_b.wait()
    b_arrive(3)
    a_arrive(1, 1)
    b_cross(7)
    a_arrive(1, 3)
    b_arrive(4)
    frame_pass(1)
    b_cross(1)
    a_arrive(1, 2)
    a_arrive(2, 0)
    b_cross(6)
    sort(zs[1])
    sort(zs[-1])
    a_arrive(2, 1)
    b_cross(2)
    a_arrive(2, 3)
    own_frames.wait()

    @pl.when(is_end)
    def _():
        for copy in mid_in_f:
            copy.wait_recv()
        pass_mid.wait_recv()

    for copy in cot_in:
        copy.wait()

    r = lax.broadcasted_iota(jnp.int32, (total, window), 0)
    w = lax.broadcasted_iota(jnp.int32, (total, window), 1)
    put = jnp.concatenate(
        [jnp.where((r - w == starts[j]) & (j < counts[0]), 1.0, 0.0).astype(BF16) for j in range(slots)],
        axis=1,
    )
    direct[...] = dot(put, cot[mp])


    def project_b(i, h):
        u = h * XS + xs[i]
        weights = wb[h, xs[i]].reshape(ZS * shard_rows, qkv_b)
        proj_b[...] += dot(ext[u // CORES, u % CORES], weights)

    for b in range(LOW - 1):
        shared.append(same(ext.at[line[b], c], sibling))
    b_cross(5)
    a_arrive(2, 2)
    sort(zs[2])
    sort(zs[-2])
    b_cross(3)
    a_arrive(3, 0)
    b_cross(4)

    @pl.when(is_end)
    def _():
        pass_far.wait_recv()

    shared.append(same(ext.at[line[LOW - 1], c], sibling))
    proj_a[...] = jnp.zeros_like(proj_a)
    proj_b[...] = jnp.zeros_like(proj_b)
    a_arrive(3, 1)
    for copy in shared:
        copy.wait_recv()
    project_b(0, 0)
    project_b(0, 1)
    a_arrive(3, 3)
    project_b(1, 0)
    a_arrive(3, 2)
    sort(zs[3])
    sort(zs[-3])
    project_b(1, 1)
    project_b(3, 0)
    project_b(3, 1)


    for s in dirs:
        for i in order:
            az[s, ZS // 2, i].wait_recv()
    sort(zs[ZS // 2])

    @pl.loop(0, MP)
    def _(u):
        weights = wa[u // XS, u % XS, :, :, :size].reshape(ZS * shard_rows, size)
        proj_a[...] += dot(ext[u // CORES, u % CORES], weights)

    parts = slab // piece
    acc = jnp.zeros((slots * window, ZS * each), F32)
    for k in range(half):
        block = cot[k // parts, :, (k % parts) * piece:(k % parts + 1) * piece]
        acc += dot(block, wide[k].reshape(ZS * each, piece), NT)
    n = lax.broadcasted_iota(jnp.int32, (ZS * each, 1), 0)
    n_to = lax.broadcasted_iota(jnp.int32, (ZS * each, ZS * each), 1)
    inner = n % (group * per_shard)
    wanted = (
        n % each // (group * per_shard) * size
        + (inner // per_shard * ZS + n // each) * per_shard + inner % per_shard
    )
    columns = jnp.where(n_to == wanted, 1.0, 0.0).astype(BF16)
    heads[...] = dot(acc.astype(BF16), columns).astype(BF16)

    for s in dirs:
        for offset in range(ZS):
            bxf[s, offset].wait_recv()
    for h in range(HIGH):
        project_b(2, h)

    low[:, :qkv_b] = proj_b[...].astype(BF16)
    low[:, qkv_b:] = proj_a[...].astype(BF16)
    rows[...] = dot(put, low[...], TN).astype(BF16)

    for j in range(slots):
        span = slice(j * window, (j + 1) * window)
        for h in range(2):
            base = h * 3 * size
            queries = rows[span, base:base + size]
            keys = rows[span, base + size:base + 2 * size]
            values = rows[span, base + 2 * size:base + 3 * size]
            grad_head = heads[span, h * size:(h + 1) * size]
            scores = dot(queries, keys, NT) * scale
            powers = jnp.exp(scores - jnp.max(scores, axis=-1, keepdims=True))
            attention = powers / jnp.sum(powers, axis=-1, keepdims=True)
            grad_values = dot(attention.astype(BF16), grad_head, TN)
            grad_attention = dot(grad_head, values, NT)
            centre = jnp.sum(attention * grad_attention, axis=-1, keepdims=True)
            grad_scores = (attention * (grad_attention - centre) * scale).astype(BF16)
            grads[span, base:base + size] = dot(grad_scores, keys).astype(BF16)
            grads[span, base + size:base + 2 * size] = dot(grad_scores, queries, TN).astype(BF16)
            grads[span, base + 2 * size:base + 3 * size] = grad_values.astype(BF16)

    placed[...] = dot(put, grads[...]).astype(BF16)

    def group_part(yl_at, c_at):
        u = yl_at * CORES + c_at
        weights_b = wb[u // XS, u % XS].reshape(ZS * shard_rows, qkv_b)
        weights_a = wa[u // XS, u % XS, :, :, :size].reshape(ZS * shard_rows, size)
        return dot(placed[...], jnp.concatenate([weights_b, weights_a], axis=1), NT)

    chunks = (edge, body)
    from_end = [[later(part.at[b, t], near.at[b - 1, t], outward) for b in (1, 2, 3)] for t in chunks]
    from_mid = [[later(part.at[b, t], across.at[3 - b, t], outward) for b in (3, 2)] for t in chunks]
    to_end = [later(part.at[0, t], home.at[t], inward) for t in chunks]

    crossing = {}

    def cross(b):
        give[b] = group_part(line[b], 1 - c).astype(BF16)
        crossing[b] = push(give.at[b], take.at[b], sibling)

    def merge(b):
        own[...] = group_part(line[b], c).astype(BF16).astype(F32)
        crossing[b].wait_recv()
        own[...] += take[b].astype(F32)
        part[b] = own[...].astype(BF16)
        if b < 2:
            @pl.when(is_end if b == 0 else is_mid)
            def _():
                direct[...] += own[...]

    def end_send(*pairs):
        @pl.when(is_end)
        def _():
            for t, b in pairs:
                from_end[t][b - 1].start()

    cross(3)
    cross(2)
    merge(3)
    end_send((0, 3))
    cross(1)
    merge(2)
    end_send((0, 2))
    cross(0)
    merge(1)
    end_send((0, 1), (1, 3), (1, 2), (1, 1))

    def add(ref, t, other_ref):
        ref[...] = (ref[...].astype(F32) + other_ref[...].astype(F32)).astype(BF16)

    def mid_out(t, b):
        from_end[t][b - 1].wait_recv()
        add(part.at[b, chunks[t]], t, near.at[b - 1, chunks[t]])
        from_mid[t][3 - b].start()

    def mid_in(t):
        from_mid[t][0].wait_recv()
        add(part.at[0, chunks[t]], t, across.at[0, chunks[t]])
        to_end[t].start()

    def finish(t):
        @pl.when(is_end)
        def _():
            to_end[t].wait_recv()
            direct[chunks[t]] += home[chunks[t]].astype(F32)

        @pl.when(is_mid)
        def _():
            from_mid[t][1].wait_recv()
            from_end[t][0].wait_recv()
            direct[chunks[t]] += (
                near[0, chunks[t]].astype(F32) + across[1, chunks[t]].astype(F32)
            )

    merge(0)

    @pl.when(is_mid)
    def _():
        mid_out(0, 3)
        mid_out(0, 2)
        mid_in(0)

    finish(0)
    tail[...] = direct[frame_count:].astype(BF16)
    carried = later(tail, tail_in, at(after, mp))

    @pl.when(jnp.logical_not(final))
    def _():
        carried.start()

    @pl.when(is_mid)
    def _():
        mid_out(1, 3)
        mid_in(1)
        mid_out(1, 2)

    for copy in copies:
        copy.wait_send()

    @pl.when(jnp.logical_not(first))
    def _():
        lent.wait_send()

    @pl.when(is_end)
    def _():
        for copy in end_out:
            copy.wait_send()

    @pl.when(is_mid)
    def _():
        for copy in (*mid_out_f, *mid_in_f, pass_out, pass_mid, pass_far):
            copy.wait_send()

    finish(1)
    result[...] = direct[:frame_count]
    rest = pl.ds(window, frame_count - window)
    done_rest = pltpu.make_async_copy(
        result.at[rest], out.at[rest], local_sems.at[MAX_LOCAL - 2]
    )
    done_rest.start()

    @pl.when(jnp.logical_not(first))
    def _():
        carried.wait_recv()
        result[:window] += tail_in[...].astype(F32)

    top = pl.ds(0, window)
    done = pltpu.make_async_copy(result.at[top], out.at[top], local_sems.at[MAX_LOCAL - 1])
    done.start()
    @pl.when(jnp.logical_not(final))
    def _():
        carried.wait_send()

    @pl.when(is_end)
    def _():
        for t in range(2):
            for copy in from_end[t]:
                copy.wait_send()

    @pl.when(is_mid)
    def _():
        for t in range(2):
            for copy in from_mid[t]:
                copy.wait_send()
            to_end[t].wait_send()

    done.wait()
    done_rest.wait()


def shards(frames, cotangent, w_qkv, w_out, starts, counts):
    frame_count, slab = frames.shape
    slots, window, width = cotangent.shape
    shard_rows, group, qkv = w_qkv.shape
    size = qkv // 3
    total = frame_count + window
    all_qkv = group * qkv
    qkv_b = all_qkv - size
    out_width = w_out.shape[0] * group * width // shard_rows
    out_rows = group * width // out_width
    smem = pl.BlockSpec(memory_space=pltpu.SMEM)
    hbm = pl.BlockSpec(memory_space=pl.ANY)
    vmem = pltpu.VMEM
    return pl.pallas_call(
        kernel,
        out_shape=jax.ShapeDtypeStruct((frame_count, slab), F32),
        in_specs=[smem, smem, hbm, hbm, pl.BlockSpec(memory_space=vmem), pl.BlockSpec(memory_space=vmem)],
        out_specs=hbm,
        scratch_shapes=[
            vmem((shard_rows, size + out_width), BF16),
            vmem((shard_rows, qkv_b), BF16),
            vmem((shard_rows, out_width), F32),
            vmem((HIGH, XS, ZS, shard_rows, size + out_width), BF16),
            vmem((HIGH, XS, ZS, shard_rows, qkv_b), BF16),
            vmem((LOW, CORES, total, slab), BF16),
            vmem((MP, slots * window, slab), BF16),
            vmem((out_rows // 2, ZS, 2 * HIGH * XS * shard_rows // out_rows, out_width), BF16),
            vmem((HIGH * XS * shard_rows, HIGH * XS * shard_rows), BF16),
            vmem((total, size), F32),
            vmem((total, qkv_b), F32),
            vmem((total, all_qkv), BF16),
            vmem((slots * window, all_qkv), BF16),
            vmem((slots * window, group * size), BF16),
            vmem((slots * window, all_qkv), BF16),
            vmem((total, all_qkv), BF16),
            vmem((total, slab), F32),
            vmem((total, slab), F32),
            vmem((LOW, total, slab), BF16),
            vmem((LOW, total, slab), BF16),
            vmem((LOW, total, slab), BF16),
            vmem((LOW - 1, total, slab), BF16),
            vmem((2, total, slab), BF16),
            vmem((total, slab), BF16),
            vmem((window, slab), BF16),
            vmem((window, slab), BF16),
            vmem((frame_count, slab), F32),
            pltpu.SemaphoreType.DMA((MAX_COPIES + MAX_MAYBE,)),
            pltpu.SemaphoreType.DMA((MAX_COPIES + MAX_MAYBE,)),
            pltpu.SemaphoreType.DMA((MAX_LOCAL,)),
        ],
        compiler_params=pltpu.CompilerParams(
            collective_id=0, has_side_effects=True, vmem_limit_bytes=56 * 2**20
        ),
    )(starts, counts, frames, cotangent.reshape(slots * window, width), w_qkv, w_out)


def solution(mesh):
    placed = (
        P("video", "mp"),
        P("video", None, None),
        P("video", "mp", None),
        P("video", "mp", None),
        P("video"),
        P("video"),
    )
    return jax.shard_map(
        shards, mesh=mesh, in_specs=placed, out_specs=P("video", "mp"), check_vma=False
    )
```
